32 devices in a mesh: dp: 8 (over z, y), rep: 4 (over x, core).
Axes of the slice: x: 2, y: 2, z: 4, core: 2. Of those that a mesh axis runs over, the one named last changes fastest.
Arguments:
- hot_ids: int32 [4096, 13], P(('dp', 'rep')), may hold values from 0 to 1023
- cold_rows: int32 [4096, 13], P(('dp', 'rep')), may hold values from 0 to 2047
- cold_owner: int32 [53248, 1], P(('dp', 'rep')), may hold values from 0 to 7; in each aligned block of 1664 rows (0 to 1663, 1664 to 3327, ...) at most 416 rows name the same one
- labels: int32 [4096], P(('dp', 'rep')), may hold values 0 or 1
- hot_table: float32 [1024, 128], replicated, may hold values from -6 to 6
- hot_backup: bfloat16 [1024, 128], replicated, may hold values from -6 to 6
- cold_table: float32 [16384, 128], P('dp'), may hold values from -6 to 6
- cold_backup: bfloat16 [16384, 128], P('dp'), may hold values from -6 to 6
- cross_down: bfloat16 [3328, 512], P(None, ('dp', 'rep')), may hold values from -0.109375 to 0.109375
- cross_up: bfloat16 [512, 3328], P(('dp', 'rep')), may hold values from -0.25 to 0.25
- cross_bias: float32 [3328], replicated, may hold values from -3 to 3
- out_weight: float32 [3328], replicated, may hold values from -0.109375 to 0.109375
Outputs:
- new_hot: float32 [1024, 128], replicated
- new_cold: float32 [16384, 128], P('dp')
The draws below stay inside these ranges and needn't reach their ends.
Inputs may be any that keep to these rules, and one draw needn't show every extreme that they name: `cold_owner`: among the 1664 lookups of one device no owner is named more than 416 times, and in some device one owner is named exactly 416 times.
All inputs are finite; a program needn't handle non-finite values. No bound on the sum of `labels` on one device may be relied on, other than what follows from the above.
Results may differ from the reference program's by a relative error of at most 0.0028.
Values may be sent and summed in bfloat16 or wider, within the bound.
No kernel may reach another device: no remote copies, remote signals or barrier semaphores. Data moves between devices by JAX's collectives and lax.ppermute only.
A program may use at most 64 MiB of HBM per device.

```python
import math
import jax
import jax.numpy as jnp
import numpy as np
from jax import lax

E = 128
NH = 13
NC = 13
R = 512
B_DEV = 128
HOT = 1024
COLD_DEV = 2048
F = 3328
BATCH = 4096
COLD_ROWS = 16384
CAP = 416
N_DP = 8
N_REP = 4


def set_ends(values, stream_key, low, largest):
    spot = [jax.random.randint(jax.random.fold_in(stream_key, axis), (), 0, length) for axis, length in enumerate(values.shape)]
    longest = values.shape.index(max(values.shape))
    beside = spot[:longest] + [(spot[longest] + 1) % values.shape[longest]] + spot[longest + 1:]
    return values.at[tuple(spot)].set(low).at[tuple(beside)].set(largest)


def steps_of(own_key, shape, cuts, smallest, high):
    level, own = 1.0, jax.random.fold_in(own_key, 6)
    for position, parts in cuts:
        heights = jnp.exp(jax.random.uniform(jax.random.fold_in(own, position), (parts,), jnp.float32, smallest / len(cuts), high / len(cuts)))
        level = level * jnp.repeat(heights, shape[position] // parts).reshape([-1 if axis == position else 1 for axis in range(len(shape))])
    return level


def rank_table(amount, skew):
    loads = [(1 << 20) // math.isqrt(grade ** skew) + 1 for grade in range(1, amount + 1)]
    scale = 1 + sum(loads) // (1 << 30)
    return np.cumsum(np.array([max(1, weight // scale) for weight in loads]))


def ranked_ids(stream_key, dims, count, skew):
    table = rank_table(count, skew)
    ticket = jax.random.randint(jax.random.fold_in(stream_key, 1), dims, 0, int(table[count - 1]))
    grade = jnp.searchsorted(jnp.asarray(table, jnp.int32), ticket, side="right")
    return jax.random.permutation(jax.random.fold_in(stream_key, 2), count)[grade].astype(jnp.int32)


def deal_out(stream_key, own, number, rows, number_of, top, bound, slope):
    sequence = jax.random.permutation(stream_key, number_of)
    crowded, common = load_shares(number_of, rows * top, bound, slope, True), load_shares(number_of, rows * top, bound, slope, False)
    places = jnp.arange(number_of)

    def named(tallies, rotation):
        used = int((tallies > 0).sum())
        fixed = max(1, used // 4)
        passed = fixed + (places - fixed + rotation * (used - fixed)) % max(1, number_of - fixed)
        return jnp.zeros((number_of,), jnp.int32).at[sequence[jnp.where(places < fixed, places, passed)]].set(jnp.asarray(tallies, jnp.int32))

    tallies = jnp.where(number % 4 == 0, named(crowded, number // 4), named(common, number - number // 4 - 1))
    mixed = jax.random.permutation(jax.random.fold_in(own, 3), number_of)
    source_of, taker = mixed[0:number_of // 2 * 2:2], mixed[1:number_of // 2 * 2:2]
    room = jnp.minimum(tallies[source_of] - 1, bound - tallies[taker]) // 2
    room = jnp.where((source_of == sequence[0]) | (taker == sequence[0]) | (tallies[taker] == 0), 0, jnp.maximum(room, 0))
    passed = jax.random.randint(jax.random.fold_in(own, 4), (number_of // 2,), 0, 1 << 20) % (room + 1)
    tallies = tallies.at[source_of].add(-passed).at[taker].add(passed)
    members = jnp.searchsorted(jnp.cumsum(tallies), jnp.arange(rows * top), side="right").astype(jnp.int32)
    grid = members.reshape(top, rows).T
    grid = grid[jax.random.permutation(jax.random.fold_in(own, 1), rows)]
    rotation = jax.random.randint(jax.random.fold_in(own, 2), (rows, 1), 0, top)
    return jnp.take_along_axis(grid, (jnp.arange(top)[None, :] + rotation) % top, axis=1)


def load_shares(number_of, total, most, slope, full):
    loads = [(1 << 20) // math.isqrt(rank ** slope) + 1 for rank in range(1, number_of + 1)]
    largest = most if full else min(most, max(-(-total // number_of), total * loads[0] // sum(loads)))
    least = 1 if total - largest >= number_of - 1 else 0
    given, rest = [largest] + [least] * (number_of - 1), total - largest - least * (number_of - 1)
    while rest > 0:
        candidates = [i for i in range(1, number_of) if given[i] < largest] or [i for i in range(1, number_of) if given[i] < most]
        pool, budget = sum([loads[i] for i in candidates]), rest
        for i in candidates:
            extra = min(most - given[i], max(1, budget * loads[i] // pool), rest)
            given[i] = given[i] + extra
            rest = rest - extra
    return np.array(given)


def noise(rng, extent, scale, most, shards=(), held_as=jnp.bfloat16):
    result = jax.random.normal(rng, extent, jnp.float32) * scale
    if len(shards) > 0:
        result = steps_of(rng, extent, shards, -0.22, 0.18) * result
    return jnp.clip(result, min=-most, max=most).astype(held_as)


def setup_inputs(seed: int = 0) -> dict:
    arg_keys = jax.random.split(jax.random.key(seed), 13)
    hot_ids = set_ends(ranked_ids(arg_keys[0], (BATCH, NH), HOT, 1), jax.random.fold_in(arg_keys[0], 3), 0, HOT - 1).astype(jnp.int32)
    cold_rows = set_ends(jax.random.randint(arg_keys[1], (BATCH, NC), 0, COLD_DEV), jax.random.fold_in(arg_keys[1], 1), 0, COLD_DEV - 1).astype(jnp.int32)
    cold_owner_keys = jax.random.split(jax.random.fold_in(arg_keys[2], 1), (BATCH * NC) // (B_DEV * NC))
    cold_owner_turns = jax.random.permutation(jax.random.fold_in(arg_keys[2], 3), (BATCH * NC) // (B_DEV * NC))
    cold_owner = jax.vmap(lambda own, number: deal_out(jax.random.fold_in(arg_keys[2], 2), own, number, B_DEV * NC, N_DP, 1, CAP, 2))(cold_owner_keys, cold_owner_turns).reshape((BATCH * NC, 1))
    labels = set_ends((jax.random.randint(arg_keys[3], (BATCH,), 0, 4) < 1).astype(jnp.int32), jax.random.fold_in(arg_keys[3], 1), 0, 1)
    hot_table = noise(arg_keys[4], (HOT, E), 1.0, 6.0, (), jnp.float32)
    hot_backup = noise(arg_keys[5], (HOT, E), 1.0, 6.0)
    cold_table = noise(arg_keys[6], (COLD_ROWS, E), 1.0, 6.0, ((0, 8),), jnp.float32)
    cold_backup = noise(arg_keys[7], (COLD_ROWS, E), 1.0, 6.0, ((0, 8),))
    cross_down = noise(arg_keys[8], (F, R), F ** -0.5, 0.109375, ((1, 32),))
    cross_up = noise(arg_keys[9], (R, F), R ** -0.5, 0.25, ((0, 32),))
    cross_bias = noise(arg_keys[10], (F,), 0.5, 3.0, (), jnp.float32)
    out_weight = noise(arg_keys[11], (F,), F ** -0.5, 0.109375, (), jnp.float32)
    return {"hot_ids": hot_ids, "cold_rows": cold_rows, "cold_owner": cold_owner, "labels": labels, "hot_table": hot_table, "hot_backup": hot_backup, "cold_table": cold_table, "cold_backup": cold_backup, "cross_down": cross_down, "cross_up": cross_up, "cross_bias": cross_bias, "out_weight": out_weight}


def block_grads(carry, inputs):
    hot_acc, cold_acc = carry
    hids, crow, cown, labs, hot_table, cold_table, cross_down, cross_up, cross_bias, out_weight = inputs
    rows = hids.shape[0]
    cold_id = (cown * COLD_DEV + crow).astype(jnp.int32)
    hot_emb = hot_table[hids].astype(jnp.bfloat16)
    cold_emb = cold_table[cold_id].astype(jnp.bfloat16)
    first = jnp.concatenate([hot_emb, cold_emb], axis=1).reshape(rows, F)
    hidden = jnp.dot(first, cross_down, preferred_element_type=jnp.float32).astype(jnp.bfloat16)
    upper = jnp.dot(hidden, cross_up, preferred_element_type=jnp.float32) + cross_bias[None, :]
    first_f = first.astype(jnp.float32)
    second = first_f * upper + first_f
    logit = lax.optimization_barrier(jnp.sum(second * out_weight[None, :], axis=1))
    delta = jax.nn.sigmoid(logit) - labs.astype(jnp.float32)
    d_second = delta[:, None] * out_weight[None, :]
    d_upper = (d_second * first_f).astype(jnp.bfloat16)
    d_hidden = jnp.dot(d_upper, cross_up.T, preferred_element_type=jnp.float32).astype(jnp.bfloat16)
    d_first = d_second * (upper + 1.0) + jnp.dot(d_hidden, cross_down.T, preferred_element_type=jnp.float32)
    grads = d_first.reshape(rows, NH + NC, E)
    hot_acc = hot_acc + jax.ops.segment_sum(grads[:, :NH].reshape(rows * NH, E), hids.reshape(-1), HOT)
    cold_low = lax.optimization_barrier(grads[:, NH:].astype(jnp.bfloat16))
    cold_acc = cold_acc + jax.ops.segment_sum(cold_low.astype(jnp.float32).reshape(rows * NC, E), cold_id.reshape(-1), COLD_ROWS)
    return (hot_acc, cold_acc)

def compensate(table, backup, grad, rate):
    step_size = rate * grad
    return table - step_size - 0.5 * step_size * step_size * (table - backup.astype(jnp.float32))

def reference(hot_ids, cold_rows, cold_owner, labels, hot_table, hot_backup, cold_table, cold_backup, cross_down, cross_up, cross_bias, out_weight):
    block = B_DEV * N_REP
    count = BATCH // block
    hids = hot_ids.reshape(count, block, NH)
    crow = cold_rows.reshape(count, block, NC)
    cown = cold_owner.reshape(count, block, NC)
    labs = labels.reshape(count, block)

    def step(carry, xs):
        return (block_grads(carry, (xs[0], xs[1], xs[2], xs[3], hot_table, cold_table, cross_down, cross_up, cross_bias, out_weight)), None)
    init = (jnp.zeros((HOT, E), jnp.float32), jnp.zeros((COLD_ROWS, E), jnp.float32))
    (hot_grad, cold_grad), unused = lax.scan(step, init, (hids, crow, cown, labs))
    rate_hot = 20.0 * math.sqrt(HOT / (BATCH * NH))
    rate_cold = 20.0 * math.sqrt(COLD_ROWS / (BATCH * NC))
    return (compensate(hot_table, hot_backup, hot_grad, rate_hot), compensate(cold_table, cold_backup, cold_grad, rate_cold))
```

```python
import math

import jax
import jax.numpy as jnp
from jax import lax
from jax.sharding import PartitionSpec as P

E = 128
NH = 13
NC = 13
HOT = 1024
F = 3328


def compensate(table, backup, grad, rate):
    step_size = rate * grad
    return table - step_size - 0.5 * step_size * step_size * (table - backup.astype(jnp.float32))


def is_small(n_data, n_reps):
    return n_reps == 4 and n_data % 2 == 0 and n_data <= 16


def swap(value, axis, distance):
    size = lax.axis_size(axis)
    return lax.ppermute(value, axis, [(i, i ^ distance) for i in range(size)])


def shift(value, axis, distance):
    size = lax.axis_size(axis)
    return lax.ppermute(value, axis, [(i, (i + distance) % size) for i in range(size)])


def gather_weights(down_t, up):
    n_data = lax.axis_size("dp")
    own = jnp.concatenate([down_t, up], axis=0)
    rank = down_t.shape[0]
    column = [own] + [shift(own, "dp", 2 * k) for k in range(1, n_data // 2)]
    half = len(column) * rank
    column = jnp.concatenate([c[:rank] for c in column] + [c[rank:] for c in column], axis=0)
    over_x = swap(column, "rep", 2)
    over_y = swap(column, "dp", 1)
    across = jnp.concatenate(
        [swap(over_y[:half], "rep", 2), swap(over_x[half:], "dp", 1)], axis=0
    )
    pieces = []
    for piece in (column, over_x, over_y, across):
        pieces += [piece, swap(piece, "rep", 1)]
    return (
        jnp.concatenate([p[:half] for p in pieces], axis=0),
        jnp.concatenate([p[half:] for p in pieces], axis=0),
    )


def half_of(value, index, count):
    rows = value.shape[0] // count
    return lax.dynamic_slice_in_dim(value, index * rows, rows, axis=0)


def paired(mine, other, index):
    return jnp.where(
        index == 0,
        jnp.concatenate([mine, other], axis=0),
        jnp.concatenate([other, mine], axis=0),
    )


def sum_hot(partial):
    n_data = lax.axis_size("dp")
    nz = n_data // 2
    rep, data = lax.axis_index("rep"), lax.axis_index("dp")
    core, x, y, z = rep % 2, rep // 2, data % 2, data // 2
    total = partial
    for axis, distance, index in (("rep", 1, core), ("rep", 2, x), ("dp", 1, y)):
        total = half_of(total, index, 2) + swap(half_of(total, 1 - index, 2), axis, distance)
    rows = total.shape[0] // nz
    parts = [half_of(total, z, nz)]
    for k in range(1, nz):
        parts.append(shift(half_of(total, (z + k) % nz, nz), "dp", 2 * k))
    total = sum(parts[1:], parts[0])
    back = [total] + [shift(total, "dp", 2 * k) for k in range(1, nz)]
    whole = jnp.zeros((rows * nz, E), total.dtype)
    for k, piece in enumerate(back):
        whole = lax.dynamic_update_slice_in_dim(whole, piece, ((z - k) % nz) * rows, axis=0)
    total = whole
    for axis, distance, index in (("dp", 1, y), ("rep", 2, x), ("rep", 1, core)):
        total = paired(total, swap(total, axis, distance), index)
    return total


def sum_cold(partial):
    rep = lax.axis_index("rep")
    core = rep % 2
    chip = partial + swap(partial, "rep", 1)
    mine = half_of(chip, core, 2).astype(jnp.bfloat16)
    mine = mine.astype(jnp.float32) + swap(mine, "rep", 2).astype(jnp.float32)
    return paired(mine, swap(mine, "rep", 1), core)


def shards(
    hot_ids,
    cold_rows,
    cold_owner,
    labels,
    hot_table,
    hot_backup,
    cold_table,
    cold_backup,
    cross_down,
    cross_up,
    cross_bias,
    out_weight,
):
    rows = hot_ids.shape[0]
    n_data = lax.axis_size("dp")
    n_reps = lax.axis_size("rep")
    lookups = rows * NC
    capacity = 2 * ((lookups + n_data - 1) // n_data)
    owned = cold_table.shape[0]
    if is_small(n_data, n_reps):
        down_t, up_full = gather_weights(cross_down.T, cross_up)
    else:
        down_t = lax.all_gather(cross_down.T, ("dp", "rep"), axis=0, tiled=True)
        up_full = lax.all_gather(cross_up, ("dp", "rep"), axis=0, tiled=True)
    owner = cold_owner.reshape(lookups)
    local_row = cold_rows.reshape(lookups)
    onehot = (owner[:, None] == jnp.arange(n_data, dtype=jnp.int32)[None, :]).astype(jnp.int32)
    running = jnp.cumsum(onehot, axis=0)
    slot = jnp.sum(onehot * running, axis=1) - 1
    place = owner * capacity + slot
    requests = (
        jnp.full((n_data * capacity,), -1, jnp.int32)
        .at[place]
        .set(local_row)
        .reshape(n_data, capacity)
    )
    asked = lax.all_to_all(requests, "dp", split_axis=0, concat_axis=0, tiled=True)
    safe = jnp.maximum(asked, 0)
    found = jnp.take(cold_table, safe, axis=0).astype(jnp.bfloat16)
    returned = lax.all_to_all(found, "dp", split_axis=0, concat_axis=0, tiled=True)
    cold_emb = returned.reshape(n_data * capacity, E)[place].reshape(rows, NC, E)
    hot_emb = hot_table[hot_ids].astype(jnp.bfloat16)
    first = jnp.concatenate([hot_emb, cold_emb], axis=1).reshape(rows, F)
    hidden = jnp.dot(first, down_t.T, preferred_element_type=jnp.float32).astype(jnp.bfloat16)
    upper = jnp.dot(hidden, up_full, preferred_element_type=jnp.float32) + cross_bias[None, :]
    first_f = first.astype(jnp.float32)
    second = first_f * upper + first_f
    logit = jnp.sum(second * out_weight[None, :], axis=1)
    delta = jax.nn.sigmoid(logit) - labels.astype(jnp.float32)
    d_second = delta[:, None] * out_weight[None, :]
    d_upper = (d_second * first_f).astype(jnp.bfloat16)
    d_hidden = jnp.dot(d_upper, up_full.T, preferred_element_type=jnp.float32).astype(jnp.bfloat16)
    d_first = d_second * (upper + 1.0) + jnp.dot(
        d_hidden, down_t, preferred_element_type=jnp.float32
    )
    grads = d_first.reshape(rows, NH + NC, E)
    hot_partial = jax.ops.segment_sum(grads[:, :NH].reshape(rows * NH, E), hot_ids.reshape(-1), HOT)
    cold_low = grads[:, NH:].astype(jnp.bfloat16).reshape(lookups, E)
    outgoing = (
        jnp.zeros((n_data * capacity, E), jnp.bfloat16)
        .at[place]
        .set(cold_low)
        .reshape(n_data, capacity, E)
    )
    incoming = lax.all_to_all(outgoing, "dp", split_axis=0, concat_axis=0, tiled=True)
    flat_ids = asked.reshape(-1)
    segment = jnp.where(flat_ids >= 0, flat_ids, owned)
    cold_partial = jax.ops.segment_sum(
        incoming.reshape(n_data * capacity, E).astype(jnp.float32), segment, owned
    )
    batch_all = rows * n_data * n_reps
    rate_hot = 20.0 * math.sqrt(HOT / (batch_all * NH))
    rate_cold = 20.0 * math.sqrt(owned * n_data / (batch_all * NC))
    if is_small(n_data, n_reps):
        hot_grad = sum_hot(hot_partial)
        cold_grad = sum_cold(cold_partial)
    else:
        hot_grad = lax.psum(hot_partial, ("dp", "rep"))
        cold_grad = lax.psum(cold_partial, "rep")
    new_hot = compensate(hot_table, hot_backup, hot_grad, rate_hot)
    new_cold = compensate(cold_table, cold_backup, cold_grad, rate_cold)
    return (new_hot, new_cold)


def solution(mesh):
    placed = (
        P(("dp", "rep"), None),
        P(("dp", "rep"), None),
        P(("dp", "rep"), None),
        P(("dp", "rep")),
        P(),
        P(),
        P("dp", None),
        P("dp", None),
        P(None, ("dp", "rep")),
        P(("dp", "rep"), None),
        P(),
        P(),
    )
    return jax.shard_map(
        shards, mesh=mesh, in_specs=placed, out_specs=(P(), P("dp", None)), check_vma=False
    )
```

```python
import functools
import math

import jax
import jax.numpy as jnp
from jax import lax
from jax.experimental import pallas as pl
from jax.experimental.pallas import tpu as pltpu
from jax.sharding import PartitionSpec as P

E = 128
NH = 13
NC = 13
HOT = 1024
F = 3328


def compensate(table, backup, grad, rate):
    step_size = rate * grad
    return table - step_size - 0.5 * step_size * step_size * (table - backup.astype(jnp.float32))


def is_small(n_data, n_reps):
    return n_reps == 4 and n_data % 2 == 0 and n_data <= 16


def swap(value, axis, distance):
    size = lax.axis_size(axis)
    return lax.ppermute(value, axis, [(i, i ^ distance) for i in range(size)])


def shift(value, axis, distance):
    size = lax.axis_size(axis)
    return lax.ppermute(value, axis, [(i, (i + distance) % size) for i in range(size)])


def weight_pieces(down_t, up):
    n_data = lax.axis_size("dp")
    own = jnp.concatenate([down_t, up], axis=0)
    rank = down_t.shape[0]
    column = [own] + [shift(own, "dp", 2 * k) for k in range(1, n_data // 2)]
    half = len(column) * rank
    column = jnp.concatenate([c[:rank] for c in column] + [c[rank:] for c in column], axis=0)
    over_x = swap(column, "rep", 2)
    over_y = swap(column, "dp", 1)
    across = jnp.concatenate(
        [swap(over_y[:half], "rep", 2), swap(over_x[half:], "dp", 1)], axis=0
    )
    pieces = []
    for piece in (column, over_x, over_y, across):
        pieces += [piece, swap(piece, "rep", 1)]
    return pieces


def half_of(value, index, count):
    rows = value.shape[0] // count
    return lax.dynamic_slice_in_dim(value, index * rows, rows, axis=0)


def paired(mine, other, index):
    return jnp.where(
        index == 0,
        jnp.concatenate([mine, other], axis=0),
        jnp.concatenate([other, mine], axis=0),
    )


def sum_hot(partial):
    n_data = lax.axis_size("dp")
    nz = n_data // 2
    rep, data = lax.axis_index("rep"), lax.axis_index("dp")
    core, x, y, z = rep % 2, rep // 2, data % 2, data // 2
    total = partial
    for axis, distance, index in (("rep", 1, core), ("rep", 2, x), ("dp", 1, y)):
        total = half_of(total, index, 2) + swap(half_of(total, 1 - index, 2), axis, distance)
    rows = total.shape[0] // nz
    parts = [half_of(total, z, nz)]
    for k in range(1, nz):
        parts.append(shift(half_of(total, (z + k) % nz, nz), "dp", 2 * k))
    total = sum(parts[1:], parts[0])
    back = [total] + [shift(total, "dp", 2 * k) for k in range(1, nz)]
    whole = jnp.zeros((rows * nz, E), total.dtype)
    for k, piece in enumerate(back):
        whole = lax.dynamic_update_slice_in_dim(whole, piece, ((z - k) % nz) * rows, axis=0)
    total = whole
    for axis, distance, index in (("dp", 1, y), ("rep", 2, x), ("rep", 1, core)):
        total = paired(total, swap(total, axis, distance), index)
    return total


def sum_cold(partial):
    rep = lax.axis_index("rep")
    core = rep % 2
    chip = partial + swap(partial, "rep", 1)
    mine = half_of(chip, core, 2).astype(jnp.bfloat16)
    mine = mine.astype(jnp.float32) + swap(mine, "rep", 2).astype(jnp.float32)
    return paired(mine, swap(mine, "rep", 1), core)


LANES = 128
GROUP = 16
BF = jnp.bfloat16
F32 = jnp.float32
VMEM = pl.BlockSpec(memory_space=pltpu.VMEM)
SMEM = pl.BlockSpec(memory_space=pltpu.SMEM)
ANY = pl.BlockSpec(memory_space=pl.ANY)
NT = (((1,), (1,)), ((), ()))


def call(body, out_shape, in_specs, scratch, cost, name, limit=40):
    flops, moved = cost
    single = not isinstance(out_shape, tuple)
    return pl.pallas_call(
        body,
        out_shape=out_shape,
        in_specs=in_specs,
        out_specs=VMEM if single else tuple([VMEM] * len(out_shape)),
        scratch_shapes=scratch,
        compiler_params=pltpu.CompilerParams(vmem_limit_bytes=limit << 20),
        cost_estimate=pl.CostEstimate(flops=flops, bytes_accessed=moved, transcendentals=0),
        name=name,
    )


def route_body(n_data, capacity, owner_ref, row_ref, place_ref, ask_ref):
    lines = owner_ref.shape[0]
    padded = place_ref.shape[0]
    blocks = ask_ref.shape[0] // n_data
    count = n_data * padded
    owner = jnp.concatenate(
        [owner_ref[...], jnp.full((padded - lines, LANES), -1, jnp.int32)], axis=0
    )
    named = jnp.concatenate([(owner == d).astype(F32) for d in range(n_data)], axis=0).astype(BF)
    at = lax.broadcasted_iota(jnp.int32, (LANES, LANES), 0)
    to = lax.broadcasted_iota(jnp.int32, (LANES, LANES), 1)
    before = (at < to).astype(F32).astype(BF)
    within = jnp.dot(named, before, preferred_element_type=F32)
    sums = jnp.dot(named, jnp.ones((LANES, LANES), BF), preferred_element_type=F32)
    line = lax.broadcasted_iota(jnp.int32, (count, count), 0)
    other = lax.broadcasted_iota(jnp.int32, (count, count), 1)
    above = ((line // padded == other // padded) & (other < line)).astype(F32).astype(BF)
    rank = within + jnp.dot(above, sums.astype(BF), preferred_element_type=F32)
    slot = jnp.zeros((padded, LANES), F32)
    for d in range(n_data):
        slot = slot + jnp.where(owner == d, rank[d * padded : (d + 1) * padded], 0.0)
    slot = slot.astype(jnp.int32)
    place_ref[...] = owner * capacity + slot
    high = owner * blocks + slot // LANES
    low = slot % LANES
    asks = ask_ref.shape[0]
    ask_line = lax.broadcasted_iota(jnp.int32, (asks, LANES), 0)
    lefts, rights = [], []
    for s in range(lines):
        hit = ask_line == high[s : s + 1]
        row = row_ref[s : s + 1]
        zero = jnp.zeros((asks, LANES), F32)
        lefts.append(
            jnp.concatenate(
                [
                    jnp.where(hit, (row // 16).astype(F32), zero),
                    jnp.where(hit, (row % 16).astype(F32), zero),
                    jnp.where(hit, 1.0, zero),
                ],
                axis=0,
            ).astype(BF)
        )
        rights.append((at == low[s : s + 1]).astype(F32).astype(BF))
    found = lax.dot_general(
        jnp.concatenate(lefts, axis=1),
        jnp.concatenate(rights, axis=1),
        NT,
        preferred_element_type=F32,
    )
    asked = found[:asks] * 16.0 + found[asks : 2 * asks] + found[2 * asks :] - 1.0
    lane = lax.broadcasted_iota(jnp.int32, (asks, LANES), 1)
    for d in range(n_data):
        total = jnp.sum(sums[d * padded : (d + 1) * padded], axis=0, keepdims=True)
        asked = jnp.where((ask_line == d * blocks + blocks - 1) & (lane == LANES - 1), total, asked)
    ask_ref[...] = asked.astype(jnp.int32)


def serve_body(n_data, capacity, ask_ref, table_ref, out_ref, found):
    blocks = ask_ref.shape[0] // n_data
    found[...] = jnp.zeros_like(found)
    for d in range(n_data):
        asked = ask_ref[d * blocks + blocks - 1, LANES - 1]

        def group(g, carry, d=d):
            line, lane = d * blocks + g // 8, (g % 8) * GROUP
            start = pl.multiple_of(d * capacity + g * GROUP, GROUP)
            for k in range(GROUP):
                row = jnp.maximum(ask_ref[line, lane + k], 0)
                found[pl.ds(start + k, 1), :] = table_ref[pl.ds(row, 1), :]
            return carry

        lax.fori_loop(0, (asked + GROUP - 1) // GROUP, group, 0)
    out_ref[...] = found[...].astype(BF)


def pick(index_ref, source, into, lines):
    def group(g, carry):
        line, lane = g // 8, (g % 8) * GROUP
        start = pl.multiple_of(g * GROUP, GROUP)
        for k in range(GROUP):
            into[pl.ds(start + k, 1), :] = source[pl.ds(index_ref[line, lane + k], 1), :]
        return carry

    lax.fori_loop(0, lines * 8, group, 0)


def hot_rows_body(id_ref, table_ref, out_ref, found):
    pick(id_ref, table_ref, found, NH)
    out_ref[...] = found[...].astype(BF)


def cross_body(
    rank,
    place_ref,
    back_ref,
    hot_ref,
    label_ref,
    bias_ref,
    weight_ref,
    *rest,
):
    n_pieces = len(rest) - 10
    pieces = rest[:n_pieces]
    send_ref, hot_grad_ref, down, up, back, cold, upper, x_all, du_all, sem = rest[n_pieces:]
    half = pieces[0].shape[0] // 2
    copies = []
    for part, target in ((0, down), (1, up)):
        for i, piece in enumerate(pieces):
            copy = pltpu.make_async_copy(
                piece.at[pl.ds(part * half, half)],
                target.at[pl.ds(i * half, half)],
                sem.at[part, i],
            )
            copy.start()
            copies.append(copy)
    back[...] = back_ref[...].astype(F32)
    pick(place_ref, back, cold, NC)
    rows = LANES
    for s in range(NH):
        x_all[:, s * E : (s + 1) * E] = hot_ref[s * rows : (s + 1) * rows, :]
    for s in range(NC):
        x_all[:, (NH + s) * E : (NH + s + 1) * E] = cold[s * rows : (s + 1) * rows, :].astype(BF)
    for copy in copies[:n_pieces]:
        copy.wait()
    hidden = lax.dot_general(x_all[...], down[...], NT, preferred_element_type=F32).astype(BF)
    for copy in copies[n_pieces:]:
        copy.wait()
    wide = 2 * E
    chunks = [pl.ds(c * wide, wide) for c in range(F // wide)]
    logit = jnp.zeros((rows, wide), F32)
    for c in chunks:
        u = jnp.dot(hidden, up[:, c], preferred_element_type=F32) + bias_ref[:, c]
        upper[:, c] = u
        x = x_all[:, c].astype(F32)
        logit = logit + (x * u + x) * weight_ref[:, c]
    logit = jnp.sum(logit, axis=1, keepdims=True)
    at = lax.broadcasted_iota(jnp.int32, (rows, rows), 0)
    to = lax.broadcasted_iota(jnp.int32, (rows, rows), 1)
    label = jnp.sum(jnp.where(at == to, label_ref[...].astype(F32), 0.0), axis=1, keepdims=True)
    delta = 1.0 / (1.0 + jnp.exp(-logit)) - label
    for c in chunks:
        du_all[:, c] = (delta * weight_ref[:, c] * x_all[:, c].astype(F32)).astype(BF)
    dh = lax.dot_general(du_all[...], up[...], NT, preferred_element_type=F32).astype(BF)
    back[...] = jnp.zeros_like(back)
    for i, c in enumerate(chunks):
        grad = delta * weight_ref[:, c] * (upper[:, c] + 1.0) + jnp.dot(
            dh, down[:, c], preferred_element_type=F32
        )
        for j in range(2):
            s = 2 * i + j
            piece = grad[:, j * E : (j + 1) * E]
            if s < NH:
                hot_grad_ref[s * rows : (s + 1) * rows, :] = piece
            else:
                cold[(s - NH) * rows : (s - NH + 1) * rows, :] = piece

    def group(g, carry):
        line, lane = g // 8, (g % 8) * GROUP
        start = pl.multiple_of(g * GROUP, GROUP)
        for k in range(GROUP):
            back[pl.ds(place_ref[line, lane + k], 1), :] = cold[pl.ds(start + k, 1), :]
        return carry

    lax.fori_loop(0, NC * 8, group, 0)
    send_ref[...] = back[...].astype(BF)


def hot_sum_body(id_ref, grad_ref, out_ref, hits):
    names = lax.broadcasted_iota(jnp.int32, (HOT, LANES), 0)
    for s in range(NH):
        hits[:, s * LANES : (s + 1) * LANES] = (names == id_ref[s : s + 1, :]).astype(F32).astype(BF)
    grad = grad_ref[...]
    first = grad.astype(BF)
    rest = (grad - first.astype(F32)).astype(BF)
    both = jnp.dot(
        hits[...], jnp.concatenate([first, rest], axis=1), preferred_element_type=F32
    )
    out_ref[...] = both[:, :E] + both[:, E:]


def cold_sum_body(n_data, capacity, ask_ref, grad_ref, out_ref, hits):
    owned = out_ref.shape[0]
    blocks = ask_ref.shape[0] // n_data
    names = lax.broadcasted_iota(jnp.int32, (owned, LANES), 0)
    for d in range(n_data):
        for b in range(blocks):
            wide = min(LANES, capacity - b * LANES)
            hit = (names == ask_ref[d * blocks + b : d * blocks + b + 1, :]).astype(F32).astype(BF)
            start = d * capacity + b * LANES
            hits[:, start : start + wide] = hit[:, :wide]
    out_ref[...] = jnp.dot(hits[...], grad_ref[...], preferred_element_type=F32)


def small_step(
    hot_ids, cold_rows, cold_owner, labels, hot_table, cold_table, cross_down, cross_up, cross_bias, out_weight
):
    rows = hot_ids.shape[0]
    n_data = lax.axis_size("dp")
    lookups = rows * NC
    capacity = 2 * ((lookups + n_data - 1) // n_data)
    owned = cold_table.shape[0]
    blocks = (capacity + LANES) // LANES
    places = n_data * capacity
    shape = jax.ShapeDtypeStruct
    owner_t = cold_owner.reshape(rows, NC).T
    place, ask = call(
        functools.partial(route_body, n_data, capacity),
        (shape((16, LANES), jnp.int32), shape((n_data * blocks, LANES), jnp.int32)),
        [VMEM, VMEM],
        [],
        (10**8, 10**5),
        "route",
    )(owner_t, cold_rows.T)
    asked = lax.all_to_all(ask, "dp", split_axis=0, concat_axis=0, tiled=True)
    pieces = weight_pieces(cross_down.T, cross_up)
    hot_t = hot_ids.T
    hot_rows = call(
        hot_rows_body,
        shape((NH * rows, E), BF),
        [SMEM, VMEM],
        [pltpu.VMEM((NH * rows, E), F32)],
        (10**6, 4 * 10**6),
        "hot_rows",
    )(hot_t, hot_table)
    found = call(
        functools.partial(serve_body, n_data, capacity),
        shape((places, E), BF),
        [SMEM, VMEM],
        [pltpu.VMEM((places, E), F32)],
        (10**6, 6 * 10**6),
        "serve",
    )(asked, cold_table)
    returned = lax.all_to_all(found, "dp", split_axis=0, concat_axis=0, tiled=True)
    rank = sum(p.shape[0] for p in pieces) // 2
    send, hot_grad = call(
        functools.partial(cross_body, rank),
        (shape((places, E), BF), shape((NH * rows, E), F32)),
        [SMEM] + [VMEM] * 5 + [ANY] * len(pieces),
        [
            pltpu.VMEM((rank, F), BF),
            pltpu.VMEM((rank, F), BF),
            pltpu.VMEM((places, E), F32),
            pltpu.VMEM((NC * rows, E), F32),
            pltpu.VMEM((rows, F), F32),
            pltpu.VMEM((rows, F), BF),
            pltpu.VMEM((rows, F), BF),
            pltpu.SemaphoreType.DMA((2, len(pieces))),
        ],
        (8 * rows * F * rank, 20 * 10**6),
        "cross",
    )(
        place,
        returned,
        hot_rows,
        labels.reshape(1, rows),
        cross_bias.reshape(1, F),
        out_weight.reshape(1, F),
        *pieces,
    )
    incoming = lax.all_to_all(send, "dp", split_axis=0, concat_axis=0, tiled=True)
    hot_partial = call(
        hot_sum_body,
        shape((HOT, E), F32),
        [VMEM, VMEM],
        [pltpu.VMEM((HOT, NH * rows), BF)],
        (2 * HOT * NH * rows * 2 * E, 5 * 10**6),
        "hot_sum",
    )(hot_t, hot_grad)
    cold_partial = call(
        functools.partial(cold_sum_body, n_data, capacity),
        shape((owned, E), F32),
        [VMEM, VMEM],
        [pltpu.VMEM((owned, places), BF)],
        (2 * owned * places * E, 5 * 10**6),
        "cold_sum",
    )(asked, incoming)
    return sum_hot(hot_partial), sum_cold(cold_partial)


def large_step(
    hot_ids, cold_rows, cold_owner, labels, hot_table, cold_table, cross_down, cross_up, cross_bias, out_weight
):
    rows = hot_ids.shape[0]
    n_data = lax.axis_size("dp")
    lookups = rows * NC
    capacity = 2 * ((lookups + n_data - 1) // n_data)
    owned = cold_table.shape[0]
    owner = cold_owner.reshape(lookups)
    local_row = cold_rows.reshape(lookups)
    onehot = (owner[:, None] == jnp.arange(n_data, dtype=jnp.int32)[None, :]).astype(jnp.int32)
    running = jnp.cumsum(onehot, axis=0)
    slot = jnp.sum(onehot * running, axis=1) - 1
    place = owner * capacity + slot
    requests = (
        jnp.full((n_data * capacity,), -1, jnp.int32)
        .at[place]
        .set(local_row)
        .reshape(n_data, capacity)
    )
    asked = lax.all_to_all(requests, "dp", split_axis=0, concat_axis=0, tiled=True)
    safe = jnp.maximum(asked, 0)
    found = jnp.take(cold_table, safe, axis=0).astype(jnp.bfloat16)
    found = jnp.where((asked >= 0)[:, :, None], found, jnp.zeros_like(found))
    returned = lax.all_to_all(found, "dp", split_axis=0, concat_axis=0, tiled=True)
    cold_emb = returned.reshape(n_data * capacity, E)[place].reshape(rows, NC, E)
    hot_emb = hot_table[hot_ids].astype(jnp.bfloat16)
    first = jnp.concatenate([hot_emb, cold_emb], axis=1).reshape(rows, F)
    down_full, up_full = (
        lax.all_gather(cross_down, ("dp", "rep"), axis=1, tiled=True),
        lax.all_gather(cross_up, ("dp", "rep"), axis=0, tiled=True),
    )
    hidden = jnp.dot(first, down_full, preferred_element_type=jnp.float32).astype(jnp.bfloat16)
    upper = jnp.dot(hidden, up_full, preferred_element_type=jnp.float32) + cross_bias[None, :]
    first_f = first.astype(jnp.float32)
    second = first_f * upper + first_f
    logit = jnp.sum(second * out_weight[None, :], axis=1)
    delta = jax.nn.sigmoid(logit) - labels.astype(jnp.float32)
    d_second = delta[:, None] * out_weight[None, :]
    d_upper = (d_second * first_f).astype(jnp.bfloat16)
    d_hidden = jnp.dot(d_upper, up_full.T, preferred_element_type=jnp.float32).astype(jnp.bfloat16)
    d_first = d_second * (upper + 1.0) + jnp.dot(
        d_hidden, down_full.T, preferred_element_type=jnp.float32
    )
    grads = d_first.reshape(rows, NH + NC, E)
    hot_partial = jax.ops.segment_sum(grads[:, :NH].reshape(rows * NH, E), hot_ids.reshape(-1), HOT)
    cold_low = grads[:, NH:].astype(jnp.bfloat16).reshape(lookups, E)
    outgoing = (
        jnp.zeros((n_data * capacity, E), jnp.bfloat16)
        .at[place]
        .set(cold_low)
        .reshape(n_data, capacity, E)
    )
    incoming = lax.all_to_all(outgoing, "dp", split_axis=0, concat_axis=0, tiled=True)
    flat_ids = asked.reshape(-1)
    segment = jnp.where(flat_ids >= 0, flat_ids, owned)
    cold_partial = jax.ops.segment_sum(
        incoming.reshape(n_data * capacity, E).astype(jnp.float32), segment, owned
    )
    return lax.psum(hot_partial, ("dp", "rep")), lax.psum(cold_partial, "rep")


def shards(
    hot_ids,
    cold_rows,
    cold_owner,
    labels,
    hot_table,
    hot_backup,
    cold_table,
    cold_backup,
    cross_down,
    cross_up,
    cross_bias,
    out_weight,
):
    rows = hot_ids.shape[0]
    owned = cold_table.shape[0]
    n_data = lax.axis_size("dp")
    n_reps = lax.axis_size("rep")
    step = small_step if is_small(n_data, n_reps) else large_step
    hot_grad, cold_grad = step(
        hot_ids,
        cold_rows,
        cold_owner,
        labels,
        hot_table,
        cold_table,
        cross_down,
        cross_up,
        cross_bias,
        out_weight,
    )
    batch_all = rows * n_data * n_reps
    rate_hot = 20.0 * math.sqrt(HOT / (batch_all * NH))
    rate_cold = 20.0 * math.sqrt(owned * n_data / (batch_all * NC))
    new_hot = compensate(hot_table, hot_backup, hot_grad, rate_hot)
    new_cold = compensate(cold_table, cold_backup, cold_grad, rate_cold)
    return (new_hot, new_cold)


def solution(mesh):
    placed = (
        P(("dp", "rep"), None),
        P(("dp", "rep"), None),
        P(("dp", "rep"), None),
        P(("dp", "rep")),
        P(),
        P(),
        P("dp", None),
        P("dp", None),
        P(None, ("dp", "rep")),
        P(("dp", "rep"), None),
        P(),
        P(),
    )
    return jax.shard_map(
        shards, mesh=mesh, in_specs=placed, out_specs=(P(), P("dp", None)), check_vma=False
    )
```

```python
import functools
import math

import jax
import jax.numpy as jnp
from jax import lax
from jax.experimental import pallas as pl
from jax.experimental.pallas import tpu as pltpu
from jax.sharding import PartitionSpec as P

E = 128
NH = 13
NC = 13
HOT = 1024
F = 3328


def compensate(table, backup, grad, rate):
    step_size = rate * grad
    return table - step_size - 0.5 * step_size * step_size * (table - backup.astype(jnp.float32))


def is_small(n_data, n_reps):
    return n_reps == 4 and n_data % 2 == 0 and n_data <= 16


def swap(value, axis, distance):
    size = lax.axis_size(axis)
    return lax.ppermute(value, axis, [(i, i ^ distance) for i in range(size)])


def shift(value, axis, distance):
    size = lax.axis_size(axis)
    return lax.ppermute(value, axis, [(i, (i + distance) % size) for i in range(size)])


def after(value, *others):
    return lax.optimization_barrier((value, *others))[0]


def swap_both(value):
    n_data, n_reps = lax.axis_size("dp"), lax.axis_size("rep")
    ways = [
        (d * n_reps + r, (d ^ 1) * n_reps + (r ^ 2)) for d in range(n_data) for r in range(n_reps)
    ]
    return lax.ppermute(value, ("dp", "rep"), ways)


def weight_starts(down_t, up):
    own = jnp.stack([down_t, up])[None]
    z = [shift(own, "dp", 2 * k) for k in range(1, lax.axis_size("dp") // 2)]
    return own, swap(own, "rep", 2), swap(own, "dp", 1), z


def weight_pieces(starts, first):
    own, own_x, own_y, z = starts
    z = jnp.concatenate(lax.optimization_barrier((*z, first))[:-1], axis=0)
    over_x = swap(jnp.concatenate([z, own_y], axis=0), "rep", 2)
    over_y = swap(z, "dp", 1)
    across = swap_both(z)
    pieces = []
    for piece in (own, own_x, own_y, z, over_y, over_x, across):
        pieces += [piece, swap(piece, "rep", 1)]
    return pieces


def half_of(value, index, count):
    rows = value.shape[0] // count
    return lax.dynamic_slice_in_dim(value, index * rows, rows, axis=0)


def paired(mine, other, index):
    return jnp.where(
        index == 0,
        jnp.concatenate([mine, other], axis=0),
        jnp.concatenate([other, mine], axis=0),
    )


def plane_swaps():
    return (
        (lambda v: swap(v, "rep", 2), 2),
        (lambda v: swap(v, "dp", 1), 1),
        (swap_both, 3),
    )


def hot_down(partial):
    nz = lax.axis_size("dp") // 2
    rep, data = lax.axis_index("rep"), lax.axis_index("dp")
    core, z, spot = rep % 2, data // 2, (rep // 2) * 2 + data % 2
    total = half_of(partial, core, 2) + swap(half_of(partial, 1 - core, 2), "rep", 1)
    total = half_of(total, spot, 4) + sum(move(half_of(total, spot ^ w, 4)) for move, w in plane_swaps())
    parts = [half_of(total, z, nz)]
    for k in range(1, nz):
        parts.append(shift(half_of(total, (z + k) % nz, nz), "dp", 2 * k))
    return sum(parts[1:], parts[0])


def hot_along_z(total):
    nz = lax.axis_size("dp") // 2
    z, rows = lax.axis_index("dp") // 2, total.shape[0]
    whole = jnp.zeros((rows * nz, E), total.dtype)
    for k in range(nz):
        piece = shift(total, "dp", 2 * k) if k else total
        whole = lax.dynamic_update_slice_in_dim(whole, piece, ((z - k) % nz) * rows, axis=0)
    return whole


def hot_up(total):
    rep, data = lax.axis_index("rep"), lax.axis_index("dp")
    core, spot, rows = rep % 2, (rep // 2) * 2 + data % 2, total.shape[0]
    whole = jnp.zeros((rows * 4, E), total.dtype)
    whole = lax.dynamic_update_slice_in_dim(whole, total, spot * rows, axis=0)
    for move, w in plane_swaps():
        whole = lax.dynamic_update_slice_in_dim(whole, move(total), (spot ^ w) * rows, axis=0)
    return paired(whole, swap(whole, "rep", 1), core)


def sum_cold(partial):
    rep = lax.axis_index("rep")
    core = rep % 2
    chip = partial + swap(partial, "rep", 1)
    mine = half_of(chip, core, 2).astype(jnp.bfloat16)
    mine = mine.astype(jnp.float32) + swap(mine, "rep", 2).astype(jnp.float32)
    return paired(mine, swap(mine, "rep", 1), core)


LANES = 128
GROUP = 32
BF = jnp.bfloat16
F32 = jnp.float32
VMEM = pl.BlockSpec(memory_space=pltpu.VMEM)
SMEM = pl.BlockSpec(memory_space=pltpu.SMEM)
ANY = pl.BlockSpec(memory_space=pl.ANY)
NT = (((1,), (1,)), ((), ()))


def call(body, out_shape, in_specs, scratch, cost, name, limit=40):
    flops, moved = cost
    single = not isinstance(out_shape, tuple)
    return pl.pallas_call(
        body,
        out_shape=out_shape,
        in_specs=in_specs,
        out_specs=VMEM if single else tuple([VMEM] * len(out_shape)),
        scratch_shapes=scratch,
        compiler_params=pltpu.CompilerParams(vmem_limit_bytes=limit << 20),
        cost_estimate=pl.CostEstimate(flops=flops, bytes_accessed=moved, transcendentals=0),
        name=name,
    )


def route_body(n_data, capacity, owner_ref, row_ref, place_ref, ask_ref):
    lines = owner_ref.shape[0]
    padded = place_ref.shape[0]
    blocks = ask_ref.shape[0] // n_data
    count = n_data * padded
    owner = jnp.concatenate(
        [owner_ref[...], jnp.full((padded - lines, LANES), -1, jnp.int32)], axis=0
    )
    named = jnp.concatenate([(owner == d).astype(F32) for d in range(n_data)], axis=0).astype(BF)
    at = lax.broadcasted_iota(jnp.int32, (LANES, LANES), 0)
    to = lax.broadcasted_iota(jnp.int32, (LANES, LANES), 1)
    before = (at < to).astype(F32).astype(BF)
    within = jnp.dot(named, before, preferred_element_type=F32)
    sums = jnp.dot(named, jnp.ones((LANES, LANES), BF), preferred_element_type=F32)
    line = lax.broadcasted_iota(jnp.int32, (count, count), 0)
    other = lax.broadcasted_iota(jnp.int32, (count, count), 1)
    above = ((line // padded == other // padded) & (other < line)).astype(F32).astype(BF)
    rank = within + jnp.dot(above, sums.astype(BF), preferred_element_type=F32)
    slot = jnp.zeros((padded, LANES), F32)
    for d in range(n_data):
        slot = slot + jnp.where(owner == d, rank[d * padded : (d + 1) * padded], 0.0)
    slot = slot.astype(jnp.int32)
    place_ref[...] = owner * capacity + slot
    high = owner * blocks + slot // LANES
    low = slot % LANES
    asks = ask_ref.shape[0]
    ask_line = lax.broadcasted_iota(jnp.int32, (asks, LANES), 0)
    lefts, rights = [], []
    for s in range(lines):
        hit = ask_line == high[s : s + 1]
        row = row_ref[s : s + 1]
        zero = jnp.zeros((asks, LANES), F32)
        lefts.append(
            jnp.concatenate(
                [
                    jnp.where(hit, (row // 16).astype(F32), zero),
                    jnp.where(hit, (row % 16).astype(F32), zero),
                ],
                axis=0,
            ).astype(BF)
        )
        rights.append((at == low[s : s + 1]).astype(F32).astype(BF))
    found = lax.dot_general(
        jnp.concatenate(lefts, axis=1),
        jnp.concatenate(rights, axis=1),
        NT,
        preferred_element_type=F32,
    )
    asked = found[:asks] * 16.0 + found[asks:]
    lane = lax.broadcasted_iota(jnp.int32, (asks, LANES), 1)
    for d in range(n_data):
        total = jnp.sum(sums[d * padded : (d + 1) * padded], axis=0, keepdims=True)
        asked = jnp.where((ask_line == d * blocks + blocks - 1) & (lane == LANES - 1), total, asked)
    ask_ref[...] = asked.astype(jnp.int32)


def serve_body(n_data, capacity, ask_ref, table_ref, out_ref, found):
    block = ask_ref.shape[0] // n_data
    found[...] = jnp.zeros_like(found)
    for d in range(n_data):

        def group(g, carry, d=d):
            start = pl.multiple_of(d * capacity + g * GROUP, GROUP)
            rows = [ask_ref[d * block + g * GROUP + k] for k in range(GROUP)]
            taken = [table_ref[pl.ds(row, 1), :] for row in rows]
            for k in range(GROUP):
                found[pl.ds(start + k, 1), :] = taken[k]
            return carry

        asked = ask_ref[(d + 1) * block - 1]
        lax.fori_loop(0, (asked + GROUP - 1) // GROUP, group, 0)
    out_ref[...] = found[...].astype(BF)


def pick(index_ref, source, into):
    def group(g, carry):
        start = pl.multiple_of(g * GROUP, GROUP)
        rows = [index_ref[start + k] for k in range(GROUP)]
        taken = [source[pl.ds(row, 1), :] for row in rows]
        for k in range(GROUP):
            into[pl.ds(start + k, 1), :] = taken[k]
        return carry

    lax.fori_loop(0, into.shape[0] // GROUP, group, 0)


def put(index_ref, source, into):
    def group(g, carry):
        start = pl.multiple_of(g * GROUP, GROUP)
        rows = [index_ref[start + k] for k in range(GROUP)]
        taken = [source[pl.ds(start + k, 1), :] for k in range(GROUP)]
        for k in range(GROUP):
            into[pl.ds(rows[k], 1), :] = taken[k]
        return carry

    lax.fori_loop(0, source.shape[0] // GROUP, group, 0)


def hot_rows_body(id_ref, table_ref, out_ref, found):
    pick(id_ref, table_ref, found)
    out_ref[...] = found[...].astype(BF)


def cross_body(
    place_ref,
    back_ref,
    hot_ref,
    label_ref,
    bias_ref,
    weight_ref,
    *rest,
):
    n_pieces = len(rest) - 10
    pieces = rest[:n_pieces]
    send_ref, hot_grad_ref, downs, ups, back, cold, upper, x_all, du_all, sem = rest[n_pieces:]
    copies = []
    for part, target in ((0, downs), (1, ups)):
        first = 0
        for i, piece in enumerate(pieces):
            count = piece.shape[0]
            copy = pltpu.make_async_copy(
                piece.at[:, part], target.at[pl.ds(first, count)], sem.at[part, i]
            )
            copy.start()
            copies.append(copy)
            first += count
    down = downs.reshape(downs.shape[0] * downs.shape[1], F)
    up = ups.reshape(ups.shape[0] * ups.shape[1], F)
    back[...] = back_ref[...].astype(F32)
    pick(place_ref, back, cold)
    rows = LANES
    for s in range(NH):
        x_all[:, s * E : (s + 1) * E] = hot_ref[s * rows : (s + 1) * rows, :]
    for s in range(NC):
        x_all[:, (NH + s) * E : (NH + s + 1) * E] = cold[s * rows : (s + 1) * rows, :].astype(BF)
    for copy in copies[:n_pieces]:
        copy.wait()
    hidden = lax.dot_general(x_all[...], down[...], NT, preferred_element_type=F32).astype(BF)
    for copy in copies[n_pieces:]:
        copy.wait()
    wide = 2 * E
    chunks = [pl.ds(c * wide, wide) for c in range(F // wide)]
    logit = jnp.zeros((rows, wide), F32)
    for c in chunks:
        u = jnp.dot(hidden, up[:, c], preferred_element_type=F32) + bias_ref[:, c]
        upper[:, c] = u
        x = x_all[:, c].astype(F32)
        logit = logit + (x * u + x) * weight_ref[:, c]
    logit = jnp.sum(logit, axis=1, keepdims=True)
    at = lax.broadcasted_iota(jnp.int32, (rows, rows), 0)
    to = lax.broadcasted_iota(jnp.int32, (rows, rows), 1)
    label = jnp.sum(jnp.where(at == to, label_ref[...].astype(F32), 0.0), axis=1, keepdims=True)
    delta = 1.0 / (1.0 + jnp.exp(-logit)) - label
    for c in chunks:
        du_all[:, c] = (delta * weight_ref[:, c] * x_all[:, c].astype(F32)).astype(BF)
    dh = lax.dot_general(du_all[...], up[...], NT, preferred_element_type=F32).astype(BF)
    back[...] = jnp.zeros_like(back)
    for i, c in enumerate(chunks):
        grad = delta * weight_ref[:, c] * (upper[:, c] + 1.0) + jnp.dot(
            dh, down[:, c], preferred_element_type=F32
        )
        for j in range(2):
            s = 2 * i + j
            piece = grad[:, j * E : (j + 1) * E]
            if s < NH:
                hot_grad_ref[s * rows : (s + 1) * rows, :] = piece
            else:
                cold[(s - NH) * rows : (s - NH + 1) * rows, :] = piece
    put(place_ref, cold, back)
    send_ref[...] = back[...].astype(BF)


def hot_sum_body(id_ref, grad_ref, out_ref, hits):
    names = lax.broadcasted_iota(jnp.int32, (HOT, LANES), 0)
    for s in range(NH):
        hits[:, s * LANES : (s + 1) * LANES] = (names == id_ref[s : s + 1, :]).astype(F32).astype(BF)
    grad = grad_ref[...]
    first = grad.astype(BF)
    rest = (grad - first.astype(F32)).astype(BF)
    both = jnp.dot(
        hits[...], jnp.concatenate([first, rest], axis=1), preferred_element_type=F32
    )
    out_ref[...] = both[:, :E] + both[:, E:]


def cold_sum_body(n_data, capacity, ask_ref, grad_ref, out_ref, hits):
    owned = out_ref.shape[0]
    blocks = ask_ref.shape[0] // n_data
    lines = []
    for d in range(n_data):
        for b in range(blocks):
            wide = min(LANES, capacity - b * LANES)
            lines.append(ask_ref[d * blocks + b : d * blocks + b + 1, :wide])
    ids = jnp.concatenate(lines, axis=1)
    names = lax.broadcasted_iota(jnp.int32, (owned, LANES), 0)
    for start in range(0, n_data * capacity, LANES):
        hits[:, start : start + LANES] = (
            (names == ids[:, start : start + LANES]).astype(F32).astype(BF)
        )
    out_ref[...] = jnp.dot(hits[...], grad_ref[...], preferred_element_type=F32)


def small_step(
    hot_ids, cold_rows, cold_owner, labels, hot_table, cold_table, cross_down, cross_up, cross_bias, out_weight
):
    rows = hot_ids.shape[0]
    n_data = lax.axis_size("dp")
    lookups = rows * NC
    capacity = 2 * ((lookups + n_data - 1) // n_data)
    owned = cold_table.shape[0]
    blocks = (capacity + LANES) // LANES
    places = n_data * capacity
    shape = jax.ShapeDtypeStruct
    owner_t = cold_owner.reshape(rows, NC).T
    place, ask = call(
        functools.partial(route_body, n_data, capacity),
        (shape((16, LANES), jnp.int32), shape((n_data * blocks, LANES), jnp.int32)),
        [VMEM, VMEM],
        [],
        (10**8, 10**5),
        "route",
    )(owner_t, cold_rows.T)
    asked = lax.all_to_all(ask, "dp", split_axis=0, concat_axis=0, tiled=True)
    starts = weight_starts(cross_down.T, cross_up)
    hot_t = hot_ids.T
    place = place.reshape(-1)
    hot_rows = call(
        hot_rows_body,
        shape((NH * rows, E), BF),
        [SMEM, VMEM],
        [pltpu.VMEM((NH * rows, E), F32)],
        (10**6, 4 * 10**6),
        "hot_rows",
    )(hot_t.reshape(-1), hot_table)
    asked = after(asked, hot_rows)
    found = call(
        functools.partial(serve_body, n_data, capacity),
        shape((places, E), BF),
        [SMEM, VMEM],
        [pltpu.VMEM((places, E), F32)],
        (10**6, 6 * 10**6),
        "serve",
    )(asked.reshape(-1), cold_table)
    returned = lax.all_to_all(found, "dp", split_axis=0, concat_axis=0, tiled=True)
    pieces = weight_pieces(starts, found)
    n_shards = sum(p.shape[0] for p in pieces)
    depth = cross_up.shape[0]
    rank = n_shards * depth
    send, hot_grad = call(
        cross_body,
        (shape((places, E), BF), shape((NH * rows, E), F32)),
        [SMEM] + [VMEM] * 5 + [ANY] * len(pieces),
        [
            pltpu.VMEM((n_shards, depth, F), BF),
            pltpu.VMEM((n_shards, depth, F), BF),
            pltpu.VMEM((places, E), F32),
            pltpu.VMEM((NC * rows, E), F32),
            pltpu.VMEM((rows, F), F32),
            pltpu.VMEM((rows, F), BF),
            pltpu.VMEM((rows, F), BF),
            pltpu.SemaphoreType.DMA((2, len(pieces))),
        ],
        (8 * rows * F * rank, 20 * 10**6),
        "cross",
    )(
        place,
        returned,
        hot_rows,
        labels.reshape(1, rows),
        cross_bias.reshape(1, F),
        out_weight.reshape(1, F),
        *pieces,
    )
    incoming = lax.all_to_all(send, "dp", split_axis=0, concat_axis=0, tiled=True)
    hot_partial = call(
        hot_sum_body,
        shape((HOT, E), F32),
        [VMEM, VMEM],
        [pltpu.VMEM((HOT, NH * rows), BF)],
        (2 * HOT * NH * rows * 2 * E, 5 * 10**6),
        "hot_sum",
    )(hot_t, hot_grad)
    hot_share = hot_along_z(hot_down(hot_partial))
    incoming = after(incoming, hot_share)
    cold_partial = call(
        functools.partial(cold_sum_body, n_data, capacity),
        shape((owned, E), F32),
        [VMEM, VMEM],
        [pltpu.VMEM((owned, places), BF)],
        (2 * owned * places * E, 5 * 10**6),
        "cold_sum",
    )(asked, incoming)
    return hot_up(hot_share), sum_cold(cold_partial)


def large_step(
    hot_ids, cold_rows, cold_owner, labels, hot_table, cold_table, cross_down, cross_up, cross_bias, out_weight
):
    rows = hot_ids.shape[0]
    n_data = lax.axis_size("dp")
    lookups = rows * NC
    capacity = 2 * ((lookups + n_data - 1) // n_data)
    owned = cold_table.shape[0]
    owner = cold_owner.reshape(lookups)
    local_row = cold_rows.reshape(lookups)
    onehot = (owner[:, None] == jnp.arange(n_data, dtype=jnp.int32)[None, :]).astype(jnp.int32)
    running = jnp.cumsum(onehot, axis=0)
    slot = jnp.sum(onehot * running, axis=1) - 1
    place = owner * capacity + slot
    requests = (
        jnp.full((n_data * capacity,), -1, jnp.int32)
        .at[place]
        .set(local_row)
        .reshape(n_data, capacity)
    )
    asked = lax.all_to_all(requests, "dp", split_axis=0, concat_axis=0, tiled=True)
    safe = jnp.maximum(asked, 0)
    found = jnp.take(cold_table, safe, axis=0).astype(jnp.bfloat16)
    found = jnp.where((asked >= 0)[:, :, None], found, jnp.zeros_like(found))
    returned = lax.all_to_all(found, "dp", split_axis=0, concat_axis=0, tiled=True)
    cold_emb = returned.reshape(n_data * capacity, E)[place].reshape(rows, NC, E)
    hot_emb = hot_table[hot_ids].astype(jnp.bfloat16)
    first = jnp.concatenate([hot_emb, cold_emb], axis=1).reshape(rows, F)
    down_full, up_full = (
        lax.all_gather(cross_down, ("dp", "rep"), axis=1, tiled=True),
        lax.all_gather(cross_up, ("dp", "rep"), axis=0, tiled=True),
    )
    hidden = jnp.dot(first, down_full, preferred_element_type=jnp.float32).astype(jnp.bfloat16)
    upper = jnp.dot(hidden, up_full, preferred_element_type=jnp.float32) + cross_bias[None, :]
    first_f = first.astype(jnp.float32)
    second = first_f * upper + first_f
    logit = jnp.sum(second * out_weight[None, :], axis=1)
    delta = jax.nn.sigmoid(logit) - labels.astype(jnp.float32)
    d_second = delta[:, None] * out_weight[None, :]
    d_upper = (d_second * first_f).astype(jnp.bfloat16)
    d_hidden = jnp.dot(d_upper, up_full.T, preferred_element_type=jnp.float32).astype(jnp.bfloat16)
    d_first = d_second * (upper + 1.0) + jnp.dot(
        d_hidden, down_full.T, preferred_element_type=jnp.float32
    )
    grads = d_first.reshape(rows, NH + NC, E)
    hot_partial = jax.ops.segment_sum(grads[:, :NH].reshape(rows * NH, E), hot_ids.reshape(-1), HOT)
    cold_low = grads[:, NH:].astype(jnp.bfloat16).reshape(lookups, E)
    outgoing = (
        jnp.zeros((n_data * capacity, E), jnp.bfloat16)
        .at[place]
        .set(cold_low)
        .reshape(n_data, capacity, E)
    )
    incoming = lax.all_to_all(outgoing, "dp", split_axis=0, concat_axis=0, tiled=True)
    flat_ids = asked.reshape(-1)
    segment = jnp.where(flat_ids >= 0, flat_ids, owned)
    cold_partial = jax.ops.segment_sum(
        incoming.reshape(n_data * capacity, E).astype(jnp.float32), segment, owned
    )
    return lax.psum(hot_partial, ("dp", "rep")), lax.psum(cold_partial, "rep")


def shards(
    hot_ids,
    cold_rows,
    cold_owner,
    labels,
    hot_table,
    hot_backup,
    cold_table,
    cold_backup,
    cross_down,
    cross_up,
    cross_bias,
    out_weight,
):
    rows = hot_ids.shape[0]
    owned = cold_table.shape[0]
    n_data = lax.axis_size("dp")
    n_reps = lax.axis_size("rep")
    step = small_step if is_small(n_data, n_reps) else large_step
    hot_grad, cold_grad = step(
        hot_ids,
        cold_rows,
        cold_owner,
        labels,
        hot_table,
        cold_table,
        cross_down,
        cross_up,
        cross_bias,
        out_weight,
    )
    batch_all = rows * n_data * n_reps
    rate_hot = 20.0 * math.sqrt(HOT / (batch_all * NH))
    rate_cold = 20.0 * math.sqrt(owned * n_data / (batch_all * NC))
    new_hot = compensate(hot_table, hot_backup, hot_grad, rate_hot)
    new_cold = compensate(cold_table, cold_backup, cold_grad, rate_cold)
    return (new_hot, new_cold)


def solution(mesh):
    placed = (
        P(("dp", "rep"), None),
        P(("dp", "rep"), None),
        P(("dp", "rep"), None),
        P(("dp", "rep")),
        P(),
        P(),
        P("dp", None),
        P("dp", None),
        P(None, ("dp", "rep")),
        P(("dp", "rep"), None),
        P(),
        P(),
    )
    return jax.shard_map(
        shards, mesh=mesh, in_specs=placed, out_specs=(P(), P("dp", None)), check_vma=False
    )
```

```python
import functools
import math

import jax
import jax.numpy as jnp
from jax import lax
from jax.experimental import pallas as pl
from jax.experimental.pallas import tpu as pltpu
from jax.sharding import PartitionSpec as P

E = 128
NH = 13
NC = 13
HOT = 1024
F = 3328


def compensate(table, backup, grad, rate):
    step_size = rate * grad
    return table - step_size - 0.5 * step_size * step_size * (table - backup.astype(jnp.float32))


def is_small(n_data, n_reps):
    return n_reps == 4 and n_data in (4, 8, 16)


def swap(value, axis, distance):
    size = lax.axis_size(axis)
    return lax.ppermute(value, axis, [(i, i ^ distance) for i in range(size)])


def shift(value, axis, distance):
    size = lax.axis_size(axis)
    return lax.ppermute(value, axis, [(i, (i + distance) % size) for i in range(size)])


def after(value, *others):
    return lax.optimization_barrier((value, *others))[0]


def swap_both(value):
    n_data, n_reps = lax.axis_size("dp"), lax.axis_size("rep")
    ways = [
        (d * n_reps + r, (d ^ 1) * n_reps + (r ^ 2)) for d in range(n_data) for r in range(n_reps)
    ]
    return lax.ppermute(value, ("dp", "rep"), ways)


def weight_starts(down_t, up):
    own = jnp.stack([down_t, up])[None]
    z = [shift(own, "dp", 2 * k) for k in range(1, lax.axis_size("dp") // 2)]
    return [own, swap(own, "rep", 2), swap(own, "dp", 1), swap_both(own)], jnp.concatenate(z, axis=0)


def weight_pieces(plane, z):
    over_x = swap(z, "rep", 2)
    over_y = swap(z, "dp", 1)
    across = swap(over_y, "rep", 2)
    pieces = []
    for piece in (*plane, z, over_x, over_y, across):
        pieces += [piece, swap(piece, "rep", 1)]
    return pieces


def half_of(value, index, count):
    rows = value.shape[0] // count
    return lax.dynamic_slice_in_dim(value, index * rows, rows, axis=0)


def paired(mine, other, index):
    return jnp.where(
        index == 0,
        jnp.concatenate([mine, other], axis=0),
        jnp.concatenate([other, mine], axis=0),
    )


def hot_early(partial):
    rep, data = lax.axis_index("rep"), lax.axis_index("dp")
    total = partial
    for axis, distance, index in (("rep", 1, rep % 2), ("rep", 2, rep // 2), ("dp", 1, data % 2)):
        total = half_of(total, index, 2) + swap(half_of(total, 1 - index, 2), axis, distance)
    return total + swap(total, "dp", 2)


def hot_late(total):
    rep, data = lax.axis_index("rep"), lax.axis_index("dp")
    distance = 4
    while distance < lax.axis_size("dp"):
        total = total + swap(total, "dp", distance)
        distance *= 2
    for axis, distance, index in (("dp", 1, data % 2), ("rep", 2, rep // 2), ("rep", 1, rep % 2)):
        total = paired(total, swap(total, axis, distance), index)
    return total


def sum_cold(partial):
    rep = lax.axis_index("rep")
    core = rep % 2
    chip = partial + swap(partial, "rep", 1)
    mine = half_of(chip, core, 2).astype(jnp.bfloat16)
    mine = mine.astype(jnp.float32) + swap(mine, "rep", 2).astype(jnp.float32)
    return paired(mine, swap(mine, "rep", 1), core)


LANES = 128
GROUP = 32
BF = jnp.bfloat16
F32 = jnp.float32
VMEM = pl.BlockSpec(memory_space=pltpu.VMEM)
SMEM = pl.BlockSpec(memory_space=pltpu.SMEM)
ANY = pl.BlockSpec(memory_space=pl.ANY)
NT = (((1,), (1,)), ((), ()))


def call(body, out_shape, in_specs, scratch, cost, name, limit=40):
    flops, moved = cost
    single = not isinstance(out_shape, tuple)
    return pl.pallas_call(
        body,
        out_shape=out_shape,
        in_specs=in_specs,
        out_specs=VMEM if single else tuple([VMEM] * len(out_shape)),
        scratch_shapes=scratch,
        compiler_params=pltpu.CompilerParams(vmem_limit_bytes=limit << 20),
        cost_estimate=pl.CostEstimate(flops=flops, bytes_accessed=moved, transcendentals=0),
        name=name,
    )


def route_body(n_data, capacity, owner_ref, row_ref, place_ref, ask_ref):
    lines = owner_ref.shape[0]
    padded = place_ref.shape[0]
    blocks = ask_ref.shape[0] // n_data
    count = n_data * padded
    owner = jnp.concatenate(
        [owner_ref[...], jnp.full((padded - lines, LANES), -1, jnp.int32)], axis=0
    )
    named = jnp.concatenate([(owner == d).astype(F32) for d in range(n_data)], axis=0).astype(BF)
    at = lax.broadcasted_iota(jnp.int32, (LANES, LANES), 0)
    to = lax.broadcasted_iota(jnp.int32, (LANES, LANES), 1)
    before = (at < to).astype(F32).astype(BF)
    within = jnp.dot(named, before, preferred_element_type=F32)
    sums = jnp.dot(named, jnp.ones((LANES, LANES), BF), preferred_element_type=F32)
    line = lax.broadcasted_iota(jnp.int32, (count, count), 0)
    other = lax.broadcasted_iota(jnp.int32, (count, count), 1)
    above = ((line // padded == other // padded) & (other < line)).astype(F32).astype(BF)
    rank = within + jnp.dot(above, sums.astype(BF), preferred_element_type=F32)
    slot = jnp.zeros((padded, LANES), F32)
    for d in range(n_data):
        slot = slot + jnp.where(owner == d, rank[d * padded : (d + 1) * padded], 0.0)
    slot = slot.astype(jnp.int32)
    place_ref[...] = owner * capacity + slot
    high = owner * blocks + slot // LANES
    low = slot % LANES
    asks = ask_ref.shape[0]
    ask_line = lax.broadcasted_iota(jnp.int32, (asks, LANES), 0)
    lefts, rights = [], []
    for s in range(lines):
        hit = ask_line == high[s : s + 1]
        row = row_ref[s : s + 1]
        zero = jnp.zeros((asks, LANES), F32)
        lefts.append(
            jnp.concatenate(
                [
                    jnp.where(hit, (row // 16).astype(F32), zero),
                    jnp.where(hit, (row % 16).astype(F32), zero),
                ],
                axis=0,
            ).astype(BF)
        )
        rights.append((at == low[s : s + 1]).astype(F32).astype(BF))
    found = lax.dot_general(
        jnp.concatenate(lefts, axis=1),
        jnp.concatenate(rights, axis=1),
        NT,
        preferred_element_type=F32,
    )
    asked = found[:asks] * 16.0 + found[asks:]
    lane = lax.broadcasted_iota(jnp.int32, (asks, LANES), 1)
    for d in range(n_data):
        total = jnp.sum(sums[d * padded : (d + 1) * padded], axis=0, keepdims=True)
        asked = jnp.where((ask_line == d * blocks + blocks - 1) & (lane == LANES - 1), total, asked)
    ask_ref[...] = asked.astype(jnp.int32)


def serve_body(n_data, capacity, ask_ref, table_ref, out_ref, found):
    block = ask_ref.shape[0] // n_data
    found[...] = jnp.zeros_like(found)
    for d in range(n_data):

        def group(g, carry, d=d):
            start = pl.multiple_of(d * capacity + g * GROUP, GROUP)
            rows = [ask_ref[d * block + g * GROUP + k] for k in range(GROUP)]
            taken = [table_ref[pl.ds(row, 1), :] for row in rows]
            for k in range(GROUP):
                found[pl.ds(start + k, 1), :] = taken[k]
            return carry

        asked = ask_ref[(d + 1) * block - 1]
        lax.fori_loop(0, (asked + GROUP - 1) // GROUP, group, 0)
    out_ref[...] = found[...].astype(BF)


def pick(index_ref, source, into):
    def group(g, carry):
        start = pl.multiple_of(g * GROUP, GROUP)
        rows = [index_ref[start + k] for k in range(GROUP)]
        taken = [source[pl.ds(row, 1), :] for row in rows]
        for k in range(GROUP):
            into[pl.ds(start + k, 1), :] = taken[k]
        return carry

    lax.fori_loop(0, into.shape[0] // GROUP, group, 0)


def put(index_ref, source, into):
    def group(g, carry):
        start = pl.multiple_of(g * GROUP, GROUP)
        rows = [index_ref[start + k] for k in range(GROUP)]
        taken = [source[pl.ds(start + k, 1), :] for k in range(GROUP)]
        for k in range(GROUP):
            into[pl.ds(rows[k], 1), :] = taken[k]
        return carry

    lax.fori_loop(0, source.shape[0] // GROUP, group, 0)


def hot_rows_body(id_ref, table_ref, out_ref, found):
    pick(id_ref, table_ref, found)
    out_ref[...] = found[...].astype(BF)


def cross_body(
    place_ref,
    back_ref,
    hot_ref,
    label_ref,
    bias_ref,
    weight_ref,
    *rest,
):
    n_pieces = len(rest) - 10
    pieces = rest[:n_pieces]
    send_ref, hot_grad_ref, downs, ups, back, cold, upper, x_all, du_all, sem = rest[n_pieces:]
    copies = []
    for part, target in ((0, downs), (1, ups)):
        first = 0
        for i, piece in enumerate(pieces):
            count = piece.shape[0]
            copy = pltpu.make_async_copy(
                piece.at[:, part], target.at[pl.ds(first, count)], sem.at[part, i]
            )
            copy.start()
            copies.append(copy)
            first += count
    down = downs.reshape(downs.shape[0] * downs.shape[1], F)
    up = ups.reshape(ups.shape[0] * ups.shape[1], F)
    back[...] = back_ref[...].astype(F32)
    pick(place_ref, back, cold)
    rows = LANES
    for s in range(NH):
        x_all[:, s * E : (s + 1) * E] = hot_ref[s * rows : (s + 1) * rows, :]
    for s in range(NC):
        x_all[:, (NH + s) * E : (NH + s + 1) * E] = cold[s * rows : (s + 1) * rows, :].astype(BF)
    for copy in copies[:n_pieces]:
        copy.wait()
    hidden = lax.dot_general(x_all[...], down[...], NT, preferred_element_type=F32).astype(BF)
    for copy in copies[n_pieces:]:
        copy.wait()
    wide = 2 * E
    chunks = [pl.ds(c * wide, wide) for c in range(F // wide)]
    logit = jnp.zeros((rows, wide), F32)
    for c in chunks:
        u = jnp.dot(hidden, up[:, c], preferred_element_type=F32) + bias_ref[:, c]
        upper[:, c] = u
        x = x_all[:, c].astype(F32)
        logit = logit + (x * u + x) * weight_ref[:, c]
    logit = jnp.sum(logit, axis=1, keepdims=True)
    at = lax.broadcasted_iota(jnp.int32, (rows, rows), 0)
    to = lax.broadcasted_iota(jnp.int32, (rows, rows), 1)
    label = jnp.sum(jnp.where(at == to, label_ref[...].astype(F32), 0.0), axis=1, keepdims=True)
    delta = 1.0 / (1.0 + jnp.exp(-logit)) - label
    for c in chunks:
        du_all[:, c] = (delta * weight_ref[:, c] * x_all[:, c].astype(F32)).astype(BF)
    dh = lax.dot_general(du_all[...], up[...], NT, preferred_element_type=F32).astype(BF)
    back[...] = jnp.zeros_like(back)
    for i, c in enumerate(chunks):
        grad = delta * weight_ref[:, c] * (upper[:, c] + 1.0) + jnp.dot(
            dh, down[:, c], preferred_element_type=F32
        )
        for j in range(2):
            s = 2 * i + j
            piece = grad[:, j * E : (j + 1) * E]
            if s < NH:
                hot_grad_ref[s * rows : (s + 1) * rows, :] = piece
            else:
                cold[(s - NH) * rows : (s - NH + 1) * rows, :] = piece
    put(place_ref, cold, back)
    send_ref[...] = back[...].astype(BF)


def hot_sum_body(id_ref, grad_ref, out_ref, hits):
    names = lax.broadcasted_iota(jnp.int32, (HOT, LANES), 0)
    for s in range(NH):
        hits[:, s * LANES : (s + 1) * LANES] = (names == id_ref[s : s + 1, :]).astype(F32).astype(BF)
    grad = grad_ref[...]
    first = grad.astype(BF)
    rest = (grad - first.astype(F32)).astype(BF)
    both = jnp.dot(
        hits[...], jnp.concatenate([first, rest], axis=1), preferred_element_type=F32
    )
    out_ref[...] = both[:, :E] + both[:, E:]


def cold_sum_body(n_data, capacity, ask_ref, grad_ref, out_ref, hits):
    owned = out_ref.shape[0]
    blocks = ask_ref.shape[0] // n_data
    lines = []
    for d in range(n_data):
        for b in range(blocks):
            wide = min(LANES, capacity - b * LANES)
            lines.append(ask_ref[d * blocks + b : d * blocks + b + 1, :wide])
    ids = jnp.concatenate(lines, axis=1)
    names = lax.broadcasted_iota(jnp.int32, (owned, LANES), 0)
    for start in range(0, n_data * capacity, LANES):
        hits[:, start : start + LANES] = (
            (names == ids[:, start : start + LANES]).astype(F32).astype(BF)
        )
    out_ref[...] = jnp.dot(hits[...], grad_ref[...], preferred_element_type=F32)


def small_step(
    hot_ids, cold_rows, cold_owner, labels, hot_table, cold_table, cross_down, cross_up, cross_bias, out_weight
):
    rows = hot_ids.shape[0]
    n_data = lax.axis_size("dp")
    lookups = rows * NC
    capacity = 2 * ((lookups + n_data - 1) // n_data)
    owned = cold_table.shape[0]
    blocks = (capacity + LANES) // LANES
    places = n_data * capacity
    shape = jax.ShapeDtypeStruct
    owner_t = cold_owner.reshape(rows, NC).T
    place, ask = call(
        functools.partial(route_body, n_data, capacity),
        (shape((16, LANES), jnp.int32), shape((n_data * blocks, LANES), jnp.int32)),
        [VMEM, VMEM],
        [],
        (1, 1),
        "route",
    )(owner_t, cold_rows.T)
    asked = lax.all_to_all(ask, "dp", split_axis=0, concat_axis=0, tiled=True)
    plane, z = weight_starts(cross_down.T, cross_up)
    hot_t = hot_ids.T
    place = place.reshape(-1)
    hot_rows = call(
        hot_rows_body,
        shape((NH * rows, E), BF),
        [SMEM, VMEM],
        [pltpu.VMEM((NH * rows, E), F32)],
        (1, 1),
        "hot_rows",
    )(hot_t.reshape(-1), hot_table)
    asked, hot_rows, z, *plane = lax.optimization_barrier((asked, hot_rows, z, *plane))
    found = call(
        functools.partial(serve_body, n_data, capacity),
        shape((places, E), BF),
        [SMEM, VMEM],
        [pltpu.VMEM((places, E), F32)],
        (1, 1),
        "serve",
    )(asked.reshape(-1), cold_table)
    returned = lax.all_to_all(found, "dp", split_axis=0, concat_axis=0, tiled=True)
    pieces = weight_pieces(plane, z)
    n_shards = sum(p.shape[0] for p in pieces)
    depth = cross_up.shape[0]
    rank = n_shards * depth
    send, hot_grad = call(
        cross_body,
        (shape((places, E), BF), shape((NH * rows, E), F32)),
        [SMEM] + [VMEM] * 5 + [ANY] * len(pieces),
        [
            pltpu.VMEM((n_shards, depth, F), BF),
            pltpu.VMEM((n_shards, depth, F), BF),
            pltpu.VMEM((places, E), F32),
            pltpu.VMEM((NC * rows, E), F32),
            pltpu.VMEM((rows, F), F32),
            pltpu.VMEM((rows, F), BF),
            pltpu.VMEM((rows, F), BF),
            pltpu.SemaphoreType.DMA((2, len(pieces))),
        ],
        (8 * rows * F * rank, 20 * 10**6),
        "cross",
        58,
    )(
        place,
        returned,
        hot_rows,
        labels.reshape(1, rows),
        cross_bias.reshape(1, F),
        out_weight.reshape(1, F),
        *pieces,
    )
    incoming = lax.all_to_all(send, "dp", split_axis=0, concat_axis=0, tiled=True)
    hot_partial = call(
        hot_sum_body,
        shape((HOT, E), F32),
        [VMEM, VMEM],
        [pltpu.VMEM((HOT, NH * rows), BF)],
        (2 * HOT * NH * rows * 2 * E, 5 * 10**6),
        "hot_sum",
    )(hot_t, hot_grad)
    hot_share = hot_early(hot_partial)
    incoming, hot_share = lax.optimization_barrier((incoming, hot_share))
    cold_partial = call(
        functools.partial(cold_sum_body, n_data, capacity),
        shape((owned, E), F32),
        [VMEM, VMEM],
        [pltpu.VMEM((owned, places), BF)],
        (2 * owned * places * E, 5 * 10**6),
        "cold_sum",
    )(asked, incoming)
    return hot_late(hot_share), sum_cold(cold_partial)


def large_step(
    hot_ids, cold_rows, cold_owner, labels, hot_table, cold_table, cross_down, cross_up, cross_bias, out_weight
):
    rows = hot_ids.shape[0]
    n_data = lax.axis_size("dp")
    lookups = rows * NC
    capacity = 2 * ((lookups + n_data - 1) // n_data)
    owned = cold_table.shape[0]
    owner = cold_owner.reshape(lookups)
    local_row = cold_rows.reshape(lookups)
    onehot = (owner[:, None] == jnp.arange(n_data, dtype=jnp.int32)[None, :]).astype(jnp.int32)
    running = jnp.cumsum(onehot, axis=0)
    slot = jnp.sum(onehot * running, axis=1) - 1
    place = owner * capacity + slot
    requests = (
        jnp.full((n_data * capacity,), -1, jnp.int32)
        .at[place]
        .set(local_row)
        .reshape(n_data, capacity)
    )
    asked = lax.all_to_all(requests, "dp", split_axis=0, concat_axis=0, tiled=True)
    safe = jnp.maximum(asked, 0)
    found = jnp.take(cold_table, safe, axis=0).astype(jnp.bfloat16)
    found = jnp.where((asked >= 0)[:, :, None], found, jnp.zeros_like(found))
    returned = lax.all_to_all(found, "dp", split_axis=0, concat_axis=0, tiled=True)
    cold_emb = returned.reshape(n_data * capacity, E)[place].reshape(rows, NC, E)
    hot_emb = hot_table[hot_ids].astype(jnp.bfloat16)
    first = jnp.concatenate([hot_emb, cold_emb], axis=1).reshape(rows, F)
    down_full, up_full = (
        lax.all_gather(cross_down, ("dp", "rep"), axis=1, tiled=True),
        lax.all_gather(cross_up, ("dp", "rep"), axis=0, tiled=True),
    )
    hidden = jnp.dot(first, down_full, preferred_element_type=jnp.float32).astype(jnp.bfloat16)
    upper = jnp.dot(hidden, up_full, preferred_element_type=jnp.float32) + cross_bias[None, :]
    first_f = first.astype(jnp.float32)
    second = first_f * upper + first_f
    logit = jnp.sum(second * out_weight[None, :], axis=1)
    delta = jax.nn.sigmoid(logit) - labels.astype(jnp.float32)
    d_second = delta[:, None] * out_weight[None, :]
    d_upper = (d_second * first_f).astype(jnp.bfloat16)
    d_hidden = jnp.dot(d_upper, up_full.T, preferred_element_type=jnp.float32).astype(jnp.bfloat16)
    d_first = d_second * (upper + 1.0) + jnp.dot(
        d_hidden, down_full.T, preferred_element_type=jnp.float32
    )
    grads = d_first.reshape(rows, NH + NC, E)
    hot_partial = jax.ops.segment_sum(grads[:, :NH].reshape(rows * NH, E), hot_ids.reshape(-1), HOT)
    cold_low = grads[:, NH:].astype(jnp.bfloat16).reshape(lookups, E)
    outgoing = (
        jnp.zeros((n_data * capacity, E), jnp.bfloat16)
        .at[place]
        .set(cold_low)
        .reshape(n_data, capacity, E)
    )
    incoming = lax.all_to_all(outgoing, "dp", split_axis=0, concat_axis=0, tiled=True)
    flat_ids = asked.reshape(-1)
    segment = jnp.where(flat_ids >= 0, flat_ids, owned)
    cold_partial = jax.ops.segment_sum(
        incoming.reshape(n_data * capacity, E).astype(jnp.float32), segment, owned
    )
    return lax.psum(hot_partial, ("dp", "rep")), lax.psum(cold_partial, "rep")


def shards(
    hot_ids,
    cold_rows,
    cold_owner,
    labels,
    hot_table,
    hot_backup,
    cold_table,
    cold_backup,
    cross_down,
    cross_up,
    cross_bias,
    out_weight,
):
    rows = hot_ids.shape[0]
    owned = cold_table.shape[0]
    n_data = lax.axis_size("dp")
    n_reps = lax.axis_size("rep")
    step = small_step if is_small(n_data, n_reps) else large_step
    hot_grad, cold_grad = step(
        hot_ids,
        cold_rows,
        cold_owner,
        labels,
        hot_table,
        cold_table,
        cross_down,
        cross_up,
        cross_bias,
        out_weight,
    )
    batch_all = rows * n_data * n_reps
    rate_hot = 20.0 * math.sqrt(HOT / (batch_all * NH))
    rate_cold = 20.0 * math.sqrt(owned * n_data / (batch_all * NC))
    new_hot = compensate(hot_table, hot_backup, hot_grad, rate_hot)
    new_cold = compensate(cold_table, cold_backup, cold_grad, rate_cold)
    return (new_hot, new_cold)


def solution(mesh):
    placed = (
        P(("dp", "rep"), None),
        P(("dp", "rep"), None),
        P(("dp", "rep"), None),
        P(("dp", "rep")),
        P(),
        P(),
        P("dp", None),
        P("dp", None),
        P(None, ("dp", "rep")),
        P(("dp", "rep"), None),
        P(),
        P(),
    )
    return jax.shard_map(
        shards, mesh=mesh, in_specs=placed, out_specs=(P(), P("dp", None)), check_vma=False
    )
```

```python
import functools
import math

import jax
import jax.numpy as jnp
from jax import lax
from jax.experimental import pallas as pl
from jax.experimental.pallas import tpu as pltpu
from jax.sharding import PartitionSpec as P

E = 128
NH = 13
NC = 13
HOT = 1024
F = 3328


def compensate(table, backup, grad, rate):
    step_size = rate * grad
    return table - step_size - 0.5 * step_size * step_size * (table - backup.astype(jnp.float32))


def is_small(n_data, n_reps):
    return n_reps == 4 and n_data == 8


def swap(value, axis, distance):
    size = lax.axis_size(axis)
    return lax.ppermute(value, axis, [(i, i ^ distance) for i in range(size)])


def shift(value, axis, distance):
    size = lax.axis_size(axis)
    return lax.ppermute(value, axis, [(i, (i + distance) % size) for i in range(size)])


def after(value, *others):
    return lax.optimization_barrier((value, *others))[0]


def swap_both(value):
    n_data, n_reps = lax.axis_size("dp"), lax.axis_size("rep")
    ways = [
        (d * n_reps + r, (d ^ 1) * n_reps + (r ^ 2)) for d in range(n_data) for r in range(n_reps)
    ]
    return lax.ppermute(value, ("dp", "rep"), ways)


def weight_starts(down_t, up):
    own = jnp.stack([down_t, up])[:, None]
    z = [swap(own, "dp", 2 * k) for k in range(1, lax.axis_size("dp") // 2)]
    over_x, over_y = swap(own, "rep", 2), swap(own, "dp", 1)
    return [own, over_x, over_y, swap_both(own)], z


def weight_pieces(plane, z):
    over_x, over_y = swap(z, "rep", 2), swap(z, "dp", 1)
    across = swap(over_y[0], "rep", 2), swap(over_x[1], "dp", 1)
    whole = [*plane, z, over_x, over_y]
    whole += [swap(piece, "rep", 1) for piece in whole]
    return whole, [(piece, swap(piece, "rep", 1)) for piece in across]


def half_of(value, index, count):
    rows = value.shape[0] // count
    return lax.dynamic_slice_in_dim(value, index * rows, rows, axis=0)


def paired(mine, other, index):
    return jnp.where(
        index == 0,
        jnp.concatenate([mine, other], axis=0),
        jnp.concatenate([other, mine], axis=0),
    )


def hot_early(partial):
    rep, data = lax.axis_index("rep"), lax.axis_index("dp")
    total = partial
    for axis, distance, index in (("rep", 1, rep % 2), ("rep", 2, rep // 2), ("dp", 1, data % 2)):
        total = half_of(total, index, 2) + swap(half_of(total, 1 - index, 2), axis, distance)
    for distance in (2, 4):
        total = total + swap(total, "dp", distance)
    return total


LANES = 128
GROUP = 32
BF = jnp.bfloat16
F32 = jnp.float32
VMEM = pl.BlockSpec(memory_space=pltpu.VMEM)
SMEM = pl.BlockSpec(memory_space=pltpu.SMEM)
ANY = pl.BlockSpec(memory_space=pl.ANY)
NT = (((1,), (1,)), ((), ()))


def call(body, out_shape, in_specs, scratch, cost, name, limit=40):
    flops, moved = cost
    single = not isinstance(out_shape, tuple)
    return pl.pallas_call(
        body,
        out_shape=out_shape,
        in_specs=in_specs,
        out_specs=VMEM if single else tuple([VMEM] * len(out_shape)),
        scratch_shapes=scratch,
        compiler_params=pltpu.CompilerParams(vmem_limit_bytes=limit << 20),
        cost_estimate=pl.CostEstimate(flops=flops, bytes_accessed=moved, transcendentals=0),
        name=name,
    )


def route_body(n_data, capacity, owner_ref, row_ref, place_ref, ask_ref):
    lines = owner_ref.shape[0]
    padded = place_ref.shape[0]
    blocks = ask_ref.shape[0] // n_data
    count = n_data * padded
    owner = jnp.concatenate(
        [owner_ref[...], jnp.full((padded - lines, LANES), -1, jnp.int32)], axis=0
    )
    named = jnp.concatenate([(owner == d).astype(F32) for d in range(n_data)], axis=0).astype(BF)
    at = lax.broadcasted_iota(jnp.int32, (LANES, LANES), 0)
    to = lax.broadcasted_iota(jnp.int32, (LANES, LANES), 1)
    before = (at < to).astype(F32).astype(BF)
    within = jnp.dot(named, before, preferred_element_type=F32)
    sums = jnp.dot(named, jnp.ones((LANES, LANES), BF), preferred_element_type=F32)
    line = lax.broadcasted_iota(jnp.int32, (count, count), 0)
    other = lax.broadcasted_iota(jnp.int32, (count, count), 1)
    above = ((line // padded == other // padded) & (other < line)).astype(F32).astype(BF)
    rank = within + jnp.dot(above, sums.astype(BF), preferred_element_type=F32)
    slot = jnp.zeros((padded, LANES), F32)
    for d in range(n_data):
        slot = slot + jnp.where(owner == d, rank[d * padded : (d + 1) * padded], 0.0)
    slot = slot.astype(jnp.int32)
    place_ref[...] = owner * capacity + slot
    high = owner * blocks + slot // LANES
    low = slot % LANES
    asks = ask_ref.shape[0]
    ask_line = lax.broadcasted_iota(jnp.int32, (asks, LANES), 0)
    lefts, rights = [], []
    for s in range(lines):
        hit = ask_line == high[s : s + 1]
        row = row_ref[s : s + 1]
        zero = jnp.zeros((asks, LANES), F32)
        lefts.append(
            jnp.concatenate(
                [
                    jnp.where(hit, (row // 16).astype(F32), zero),
                    jnp.where(hit, (row % 16).astype(F32), zero),
                ],
                axis=0,
            ).astype(BF)
        )
        rights.append((at == low[s : s + 1]).astype(F32).astype(BF))
    found = lax.dot_general(
        jnp.concatenate(lefts, axis=1),
        jnp.concatenate(rights, axis=1),
        NT,
        preferred_element_type=F32,
    )
    asked = found[:asks] * 16.0 + found[asks:]
    lane = lax.broadcasted_iota(jnp.int32, (asks, LANES), 1)
    for d in range(n_data):
        total = jnp.sum(sums[d * padded : (d + 1) * padded], axis=0, keepdims=True)
        asked = jnp.where((ask_line == d * blocks + blocks - 1) & (lane == LANES - 1), total, asked)
    ask_ref[...] = asked.astype(jnp.int32)


def serve_body(n_data, capacity, ask_ref, table_ref, out_ref, found):
    block = ask_ref.shape[0] // n_data
    found[...] = jnp.zeros_like(found)
    for d in range(n_data):

        def group(g, carry, d=d):
            start = pl.multiple_of(d * capacity + g * GROUP, GROUP)
            rows = [ask_ref[d * block + g * GROUP + k] for k in range(GROUP)]
            taken = [table_ref[pl.ds(row, 1), :] for row in rows]
            for k in range(GROUP):
                found[pl.ds(start + k, 1), :] = taken[k]
            return carry

        asked = ask_ref[(d + 1) * block - 1]
        lax.fori_loop(0, (asked + GROUP - 1) // GROUP, group, 0)
    out_ref[...] = found[...].astype(BF)


def pick(index_ref, source, into):
    def group(g, carry):
        start = pl.multiple_of(g * GROUP, GROUP)
        rows = [index_ref[start + k] for k in range(GROUP)]
        taken = [source[pl.ds(row, 1), :] for row in rows]
        for k in range(GROUP):
            into[pl.ds(start + k, 1), :] = taken[k]
        return carry

    lax.fori_loop(0, into.shape[0] // GROUP, group, 0)


def hot_rows_body(id_ref, table_ref, out_ref, found):
    pick(id_ref, table_ref, found)
    out_ref[...] = found[...].astype(BF)


def cross_body(
    place_ref,
    id_ref,
    back_ref,
    hot_ref,
    label_ref,
    bias_ref,
    weight_ref,
    *rest,
):
    n_pieces = len(rest) - 12
    pieces = rest[:n_pieces]
    send_ref, hot_sum_ref, downs, ups, back, cold, upper, x_all, du_all, hits, hot_grad, sem = rest[
        n_pieces:
    ]
    copies = []
    whole = [piece for piece in pieces if len(piece.shape) == 4]
    parts = [piece for piece in pieces if len(piece.shape) == 3]
    n_parts = len(parts) // 2
    for part, target in ((0, downs), (1, ups)):
        sources = [piece.at[part] for piece in whole]
        sources += parts[part * n_parts : (part + 1) * n_parts]
        first = 0
        for i, source in enumerate(sources):
            count = source.shape[0]
            copy = pltpu.make_async_copy(source, target.at[pl.ds(first, count)], sem.at[part, i])
            copy.start()
            copies.append(copy)
            first += count
    n_copies = len(copies) // 2
    down = downs.reshape(downs.shape[0] * downs.shape[1], F)
    up = ups.reshape(ups.shape[0] * ups.shape[1], F)
    names = lax.broadcasted_iota(jnp.int32, (HOT, LANES), 0)
    for s in range(NH):
        hits[:, s * LANES : (s + 1) * LANES] = (names == id_ref[s : s + 1, :]).astype(F32).astype(BF)
    back[...] = back_ref[...].astype(F32)
    pick(place_ref, back, cold)
    rows = LANES
    for s in range(NH):
        x_all[:, s * E : (s + 1) * E] = hot_ref[s * rows : (s + 1) * rows, :]
    for s in range(NC):
        x_all[:, (NH + s) * E : (NH + s + 1) * E] = cold[s * rows : (s + 1) * rows, :].astype(BF)
    for copy in copies[:n_copies]:
        copy.wait()
    hidden = lax.dot_general(x_all[...], down[...], NT, preferred_element_type=F32).astype(BF)
    for copy in copies[n_copies:]:
        copy.wait()
    wide = 2 * E
    chunks = [pl.ds(c * wide, wide) for c in range(F // wide)]
    logit = jnp.zeros((rows, wide), F32)
    for c in chunks:
        u = jnp.dot(hidden, up[:, c], preferred_element_type=F32) + bias_ref[c][None, :]
        upper[:, c] = u
        x = x_all[:, c].astype(F32)
        logit = logit + (x * u + x) * weight_ref[c][None, :]
    logit = jnp.sum(logit, axis=1, keepdims=True)
    at = lax.broadcasted_iota(jnp.int32, (rows, rows), 0)
    to = lax.broadcasted_iota(jnp.int32, (rows, rows), 1)
    label = jnp.sum(jnp.where(at == to, label_ref[...].astype(F32), 0.0), axis=1, keepdims=True)
    delta = 1.0 / (1.0 + jnp.exp(-logit)) - label
    for c in chunks:
        du_all[:, c] = (delta * weight_ref[c][None, :] * x_all[:, c].astype(F32)).astype(BF)
    dh = lax.dot_general(du_all[...], up[...], NT, preferred_element_type=F32).astype(BF)
    back[...] = jnp.zeros_like(back)
    for i, c in enumerate(chunks):
        grad = delta * weight_ref[c][None, :] * (upper[:, c] + 1.0) + jnp.dot(
            dh, down[:, c], preferred_element_type=F32
        )
        for j in range(2):
            s = 2 * i + j
            piece = grad[:, j * E : (j + 1) * E]
            if s < NH:
                first = piece.astype(BF)
                hot_grad[s * rows : (s + 1) * rows, :E] = first
                hot_grad[s * rows : (s + 1) * rows, E:] = (piece - first.astype(F32)).astype(BF)
            else:
                start = (s - NH) * rows
                cold[start : start + rows, :] = piece
                for k in range(start, start + rows):
                    back[pl.ds(place_ref[k], 1), :] = cold[pl.ds(k, 1), :]
    send_ref[...] = back[...].astype(BF)
    both = jnp.dot(hits[...], hot_grad[...], preferred_element_type=F32)
    hot_sum_ref[...] = both[:, :E] + both[:, E:]


def cold_sum_body(n_data, capacity, first_ref, ask_ref, grad_ref, out_ref, hits):
    owned = out_ref.shape[0]
    blocks = ask_ref.shape[0] // n_data
    lines = []
    for d in range(n_data):
        for b in range(blocks):
            wide = min(LANES, capacity - b * LANES)
            lines.append(ask_ref[d * blocks + b : d * blocks + b + 1, :wide])
    ids = jnp.concatenate(lines, axis=1)
    names = lax.broadcasted_iota(jnp.int32, (owned, LANES), 0) + first_ref[0]
    for start in range(0, n_data * capacity, LANES):
        hits[:, start : start + LANES] = (
            (names == ids[:, start : start + LANES]).astype(F32).astype(BF)
        )
    out_ref[...] = jnp.dot(hits[...], grad_ref[...], preferred_element_type=F32)


def small_step(
    hot_ids, cold_rows, cold_owner, labels, hot_table, cold_table, cross_down, cross_up, cross_bias, out_weight
):
    rows = hot_ids.shape[0]
    n_data = lax.axis_size("dp")
    lookups = rows * NC
    capacity = 2 * ((lookups + n_data - 1) // n_data)
    owned = cold_table.shape[0]
    blocks = (capacity + LANES) // LANES
    places = n_data * capacity
    shape = jax.ShapeDtypeStruct
    owner_t = cold_owner.reshape(rows, NC).T
    place, ask = call(
        functools.partial(route_body, n_data, capacity),
        (shape((16, LANES), jnp.int32), shape((n_data * blocks, LANES), jnp.int32)),
        [VMEM, VMEM],
        [],
        (1, 1),
        "route",
    )(owner_t, cold_rows.T)
    asked = lax.all_to_all(ask, "dp", split_axis=0, concat_axis=0, tiled=True)
    hot_t = hot_ids.T
    place = place.reshape(-1)
    hot_rows = call(
        hot_rows_body,
        shape((NH * rows, E), BF),
        [SMEM, VMEM],
        [pltpu.VMEM((NH * rows, E), F32)],
        (1, 1),
        "hot_rows",
    )(hot_t.reshape(-1), hot_table)
    plane, z = weight_starts(cross_down.T, cross_up)
    asked = after(asked, hot_rows, *plane)
    z = jnp.concatenate(lax.optimization_barrier((*z, asked))[:-1], axis=1)
    found = call(
        functools.partial(serve_body, n_data, capacity),
        shape((places, E), BF),
        [SMEM, VMEM],
        [pltpu.VMEM((places, E), F32)],
        (1, 1),
        "serve",
    )(asked.reshape(-1), cold_table)
    returned = lax.all_to_all(found, "dp", split_axis=0, concat_axis=0, tiled=True)
    whole, (down_rest, up_rest) = weight_pieces(plane, z)
    pieces = [*whole, *down_rest, *up_rest]
    n_shards = sum(p.shape[-3] for p in (*whole, *down_rest))
    depth = cross_up.shape[0]
    rank = n_shards * depth
    send, hot_partial = call(
        cross_body,
        (shape((places, E), BF), shape((HOT, E), F32)),
        [SMEM] + [VMEM] * 6 + [ANY] * len(pieces),
        [
            pltpu.VMEM((n_shards, depth, F), BF),
            pltpu.VMEM((n_shards, depth, F), BF),
            pltpu.VMEM((places, E), F32),
            pltpu.VMEM((NC * rows, E), F32),
            pltpu.VMEM((rows, F), F32),
            pltpu.VMEM((rows, F), BF),
            pltpu.VMEM((rows, F), BF),
            pltpu.VMEM((HOT, NH * rows), BF),
            pltpu.VMEM((NH * rows, 2 * E), BF),
            pltpu.SemaphoreType.DMA((2, len(whole) + len(down_rest))),
        ],
        (8 * rows * F * rank, 20 * 10**6),
        "cross",
        58,
    )(
        place,
        hot_t,
        returned,
        hot_rows,
        labels.reshape(1, rows),
        cross_bias,
        out_weight,
        *pieces,
    )
    incoming = lax.all_to_all(send, "dp", split_axis=0, concat_axis=0, tiled=True)
    hot_share = hot_early(hot_partial)
    core = lax.axis_index("rep") % 2
    incoming, hot_share = lax.optimization_barrier((incoming, hot_share))

    def cold_sum(rows_of, grads):
        return call(
            functools.partial(cold_sum_body, n_data, capacity),
            shape((owned // 2, E), F32),
            [SMEM, VMEM, VMEM],
            [pltpu.VMEM((owned // 2, places), BF)],
            (10**9, 10**7),
            "cold_sum",
        )((rows_of * (owned // 2)).reshape(1), asked, grads)

    others = cold_sum(1 - core, incoming)
    incoming = after(incoming, others)
    mine = cold_sum(core, incoming)
    hot_share = paired(hot_share, swap(hot_share, "dp", 1), lax.axis_index("dp") % 2)
    mine = (mine + swap(others, "rep", 1)).astype(BF)
    mine, hot_share = lax.optimization_barrier((mine, hot_share))
    mine = mine.astype(F32) + swap(mine, "rep", 2).astype(F32)
    hot_share = paired(hot_share, swap(hot_share, "rep", 2), lax.axis_index("rep") // 2)
    return tuple(paired(half, swap(half, "rep", 1), core) for half in (hot_share, mine))


def large_step(
    hot_ids, cold_rows, cold_owner, labels, hot_table, cold_table, cross_down, cross_up, cross_bias, out_weight
):
    rows = hot_ids.shape[0]
    n_data = lax.axis_size("dp")
    lookups = rows * NC
    capacity = 2 * ((lookups + n_data - 1) // n_data)
    owned = cold_table.shape[0]
    owner = cold_owner.reshape(lookups)
    local_row = cold_rows.reshape(lookups)
    onehot = (owner[:, None] == jnp.arange(n_data, dtype=jnp.int32)[None, :]).astype(jnp.int32)
    running = jnp.cumsum(onehot, axis=0)
    slot = jnp.sum(onehot * running, axis=1) - 1
    place = owner * capacity + slot
    requests = (
        jnp.full((n_data * capacity,), -1, jnp.int32)
        .at[place]
        .set(local_row)
        .reshape(n_data, capacity)
    )
    asked = lax.all_to_all(requests, "dp", split_axis=0, concat_axis=0, tiled=True)
    safe = jnp.maximum(asked, 0)
    found = jnp.take(cold_table, safe, axis=0).astype(jnp.bfloat16)
    found = jnp.where((asked >= 0)[:, :, None], found, jnp.zeros_like(found))
    returned = lax.all_to_all(found, "dp", split_axis=0, concat_axis=0, tiled=True)
    cold_emb = returned.reshape(n_data * capacity, E)[place].reshape(rows, NC, E)
    hot_emb = hot_table[hot_ids].astype(jnp.bfloat16)
    first = jnp.concatenate([hot_emb, cold_emb], axis=1).reshape(rows, F)
    down_full, up_full = (
        lax.all_gather(cross_down, ("dp", "rep"), axis=1, tiled=True),
        lax.all_gather(cross_up, ("dp", "rep"), axis=0, tiled=True),
    )
    hidden = jnp.dot(first, down_full, preferred_element_type=jnp.float32).astype(jnp.bfloat16)
    upper = jnp.dot(hidden, up_full, preferred_element_type=jnp.float32) + cross_bias[None, :]
    first_f = first.astype(jnp.float32)
    second = first_f * upper + first_f
    logit = jnp.sum(second * out_weight[None, :], axis=1)
    delta = jax.nn.sigmoid(logit) - labels.astype(jnp.float32)
    d_second = delta[:, None] * out_weight[None, :]
    d_upper = (d_second * first_f).astype(jnp.bfloat16)
    d_hidden = jnp.dot(d_upper, up_full.T, preferred_element_type=jnp.float32).astype(jnp.bfloat16)
    d_first = d_second * (upper + 1.0) + jnp.dot(
        d_hidden, down_full.T, preferred_element_type=jnp.float32
    )
    grads = d_first.reshape(rows, NH + NC, E)
    hot_partial = jax.ops.segment_sum(grads[:, :NH].reshape(rows * NH, E), hot_ids.reshape(-1), HOT)
    cold_low = grads[:, NH:].astype(jnp.bfloat16).reshape(lookups, E)
    outgoing = (
        jnp.zeros((n_data * capacity, E), jnp.bfloat16)
        .at[place]
        .set(cold_low)
        .reshape(n_data, capacity, E)
    )
    incoming = lax.all_to_all(outgoing, "dp", split_axis=0, concat_axis=0, tiled=True)
    flat_ids = asked.reshape(-1)
    segment = jnp.where(flat_ids >= 0, flat_ids, owned)
    cold_partial = jax.ops.segment_sum(
        incoming.reshape(n_data * capacity, E).astype(jnp.float32), segment, owned
    )
    return lax.psum(hot_partial, ("dp", "rep")), lax.psum(cold_partial, "rep")


def shards(
    hot_ids,
    cold_rows,
    cold_owner,
    labels,
    hot_table,
    hot_backup,
    cold_table,
    cold_backup,
    cross_down,
    cross_up,
    cross_bias,
    out_weight,
):
    rows = hot_ids.shape[0]
    owned = cold_table.shape[0]
    n_data = lax.axis_size("dp")
    n_reps = lax.axis_size("rep")
    step = small_step if is_small(n_data, n_reps) else large_step
    hot_grad, cold_grad = step(
        hot_ids,
        cold_rows,
        cold_owner,
        labels,
        hot_table,
        cold_table,
        cross_down,
        cross_up,
        cross_bias,
        out_weight,
    )
    batch_all = rows * n_data * n_reps
    rate_hot = 20.0 * math.sqrt(HOT / (batch_all * NH))
    rate_cold = 20.0 * math.sqrt(owned * n_data / (batch_all * NC))
    new_hot = compensate(hot_table, hot_backup, hot_grad, rate_hot)
    new_cold = compensate(cold_table, cold_backup, cold_grad, rate_cold)
    return (new_hot, new_cold)


def solution(mesh):
    placed = (
        P(("dp", "rep"), None),
        P(("dp", "rep"), None),
        P(("dp", "rep"), None),
        P(("dp", "rep")),
        P(),
        P(),
        P("dp", None),
        P("dp", None),
        P(None, ("dp", "rep")),
        P(("dp", "rep"), None),
        P(),
        P(),
    )
    return jax.shard_map(
        shards, mesh=mesh, in_specs=placed, out_specs=(P(), P("dp", None)), check_vma=False
    )
```

```python
import functools
import math

import jax
import jax.numpy as jnp
from jax import lax
from jax.experimental import pallas as pl
from jax.experimental.pallas import tpu as pltpu
from jax.sharding import PartitionSpec as P

E = 128
NH = 13
NC = 13
HOT = 1024
F = 3328


def compensate(table, backup, grad, rate):
    step_size = rate * grad
    return table - step_size - 0.5 * step_size * step_size * (table - backup.astype(jnp.float32))


def is_small(n_data, n_reps):
    return n_reps == 4 and n_data == 8


def swap(value, axis, distance):
    size = lax.axis_size(axis)
    return lax.ppermute(value, axis, [(i, i ^ distance) for i in range(size)])


def shift(value, axis, distance):
    size = lax.axis_size(axis)
    return lax.ppermute(value, axis, [(i, (i + distance) % size) for i in range(size)])


def after(value, *others):
    return lax.optimization_barrier((value, *others))[0]


def swap_both(value):
    n_data, n_reps = lax.axis_size("dp"), lax.axis_size("rep")
    ways = [
        (d * n_reps + r, (d ^ 1) * n_reps + (r ^ 2)) for d in range(n_data) for r in range(n_reps)
    ]
    return lax.ppermute(value, ("dp", "rep"), ways)


def weight_starts(down_t, up):
    own = jnp.stack([down_t, up])[:, None]
    z = [swap(own, "dp", 2 * k) for k in range(1, lax.axis_size("dp") // 2)]
    over_x, over_y = swap(own, "rep", 2), swap(own, "dp", 1)
    return [own, over_x, over_y, swap_both(own)], z


def weight_pieces(plane, z):
    over_x, over_y = swap(z, "rep", 2), swap(z, "dp", 1)
    across = swap(over_y[0], "rep", 2), swap(over_x[1], "dp", 1)
    whole = [*plane, z, over_x, over_y]
    whole += [swap(piece, "rep", 1) for piece in whole]
    return whole, [(piece, swap(piece, "rep", 1)) for piece in across]


def half_of(value, index, count):
    rows = value.shape[0] // count
    return lax.dynamic_slice_in_dim(value, index * rows, rows, axis=0)


def paired(mine, other, index):
    return jnp.where(
        index == 0,
        jnp.concatenate([mine, other], axis=0),
        jnp.concatenate([other, mine], axis=0),
    )


def hot_early(mine, other):
    total = mine + swap(other, "rep", 1)
    for axis, distance, index in (
        ("rep", 2, lax.axis_index("rep") // 2),
        ("dp", 1, lax.axis_index("dp") % 2),
    ):
        total = half_of(total, index, 2) + swap(half_of(total, 1 - index, 2), axis, distance)
    for distance in (2, 4):
        total = total + swap(total, "dp", distance)
    return total


LANES = 128
GROUP = 32
BF = jnp.bfloat16
F32 = jnp.float32
VMEM = pl.BlockSpec(memory_space=pltpu.VMEM)
SMEM = pl.BlockSpec(memory_space=pltpu.SMEM)
ANY = pl.BlockSpec(memory_space=pl.ANY)
NT = (((1,), (1,)), ((), ()))


def call(body, out_shape, in_specs, scratch, cost, name, limit=40):
    flops, moved = cost
    single = not isinstance(out_shape, tuple)
    return pl.pallas_call(
        body,
        out_shape=out_shape,
        in_specs=in_specs,
        out_specs=VMEM if single else tuple([VMEM] * len(out_shape)),
        scratch_shapes=scratch,
        compiler_params=pltpu.CompilerParams(vmem_limit_bytes=limit << 20),
        cost_estimate=pl.CostEstimate(flops=flops, bytes_accessed=moved, transcendentals=0),
        name=name,
    )


def route_body(n_data, capacity, owner_ref, row_ref, place_ref, ask_ref):
    lines = owner_ref.shape[0]
    padded = place_ref.shape[0]
    blocks = ask_ref.shape[0] // n_data
    count = n_data * padded
    owner = jnp.concatenate(
        [owner_ref[...], jnp.full((padded - lines, LANES), -1, jnp.int32)], axis=0
    )
    named = jnp.concatenate([(owner == d).astype(F32) for d in range(n_data)], axis=0).astype(BF)
    at = lax.broadcasted_iota(jnp.int32, (LANES, LANES), 0)
    to = lax.broadcasted_iota(jnp.int32, (LANES, LANES), 1)
    before = (at < to).astype(F32).astype(BF)
    within = jnp.dot(named, before, preferred_element_type=F32)
    sums = jnp.dot(named, jnp.ones((LANES, LANES), BF), preferred_element_type=F32)
    line = lax.broadcasted_iota(jnp.int32, (count, count), 0)
    other = lax.broadcasted_iota(jnp.int32, (count, count), 1)
    above = ((line // padded == other // padded) & (other < line)).astype(F32).astype(BF)
    rank = within + jnp.dot(above, sums.astype(BF), preferred_element_type=F32)
    slot = jnp.zeros((padded, LANES), F32)
    for d in range(n_data):
        slot = slot + jnp.where(owner == d, rank[d * padded : (d + 1) * padded], 0.0)
    slot = slot.astype(jnp.int32)
    place_ref[...] = owner * capacity + slot
    high = owner * blocks + slot // LANES
    low = slot % LANES
    asks = ask_ref.shape[0]
    ask_line = lax.broadcasted_iota(jnp.int32, (asks, LANES), 0)
    lefts, rights = [], []
    for s in range(lines):
        hit = ask_line == high[s : s + 1]
        row = row_ref[s : s + 1]
        zero = jnp.zeros((asks, LANES), F32)
        lefts.append(
            jnp.concatenate(
                [
                    jnp.where(hit, (row // 16).astype(F32), zero),
                    jnp.where(hit, (row % 16).astype(F32), zero),
                ],
                axis=0,
            ).astype(BF)
        )
        rights.append((at == low[s : s + 1]).astype(F32).astype(BF))
    found = lax.dot_general(
        jnp.concatenate(lefts, axis=1),
        jnp.concatenate(rights, axis=1),
        NT,
        preferred_element_type=F32,
    )
    asked = found[:asks] * 16.0 + found[asks:]
    lane = lax.broadcasted_iota(jnp.int32, (asks, LANES), 1)
    for d in range(n_data):
        total = jnp.sum(sums[d * padded : (d + 1) * padded], axis=0, keepdims=True)
        asked = jnp.where((ask_line == d * blocks + blocks - 1) & (lane == LANES - 1), total, asked)
    ask_ref[...] = asked.astype(jnp.int32)


def serve_body(n_data, capacity, ask_ref, table_ref, out_ref, found):
    block = ask_ref.shape[0] // n_data
    found[...] = jnp.zeros_like(found)
    for d in range(n_data):

        def group(g, carry, d=d):
            start = pl.multiple_of(d * capacity + g * GROUP, GROUP)
            rows = [ask_ref[d * block + g * GROUP + k] for k in range(GROUP)]
            taken = [table_ref[pl.ds(row, 1), :] for row in rows]
            for k in range(GROUP):
                found[pl.ds(start + k, 1), :] = taken[k]
            return carry

        asked = ask_ref[(d + 1) * block - 1]
        lax.fori_loop(0, (asked + GROUP - 1) // GROUP, group, 0)
    out_ref[...] = found[...].astype(BF)


def pick(index_ref, source, into):
    def group(g, carry):
        start = pl.multiple_of(g * GROUP, GROUP)
        rows = [index_ref[start + k] for k in range(GROUP)]
        taken = [source[pl.ds(row, 1), :] for row in rows]
        for k in range(GROUP):
            into[pl.ds(start + k, 1), :] = taken[k]
        return carry

    lax.fori_loop(0, into.shape[0] // GROUP, group, 0)


def hot_rows_body(id_ref, table_ref, out_ref, found):
    pick(id_ref, table_ref, found)
    out_ref[...] = found[...].astype(BF)


def cross_body(
    core_ref,
    place_ref,
    id_ref,
    back_ref,
    hot_ref,
    label_ref,
    bias_ref,
    weight_ref,
    *rest,
):
    n_pieces = len(rest) - 13
    pieces = rest[:n_pieces]
    send_ref, hot_other_ref, hot_mine_ref, *scratch = rest[n_pieces:]
    downs, ups, back, cold, upper, x_all, du_all, hits, hot_grad, sem = scratch
    copies = []
    whole = [piece for piece in pieces if len(piece.shape) == 4]
    parts = [piece for piece in pieces if len(piece.shape) == 3]
    n_parts = len(parts) // 2
    for part, target in ((0, downs), (1, ups)):
        sources = [piece.at[part] for piece in whole]
        sources += parts[part * n_parts : (part + 1) * n_parts]
        first = 0
        for i, source in enumerate(sources):
            count = source.shape[0]
            copy = pltpu.make_async_copy(source, target.at[pl.ds(first, count)], sem.at[part, i])
            copy.start()
            copies.append(copy)
            first += count
    n_copies = len(copies) // 2
    down = downs.reshape(downs.shape[0] * downs.shape[1], F)
    up = ups.reshape(ups.shape[0] * ups.shape[1], F)
    names = lax.broadcasted_iota(jnp.int32, (HOT, LANES), 0)
    for s in range(NH):
        hits[:, s * LANES : (s + 1) * LANES] = (names == id_ref[s : s + 1, :]).astype(F32).astype(BF)
    back[...] = back_ref[...].astype(F32)
    pick(place_ref, back, cold)
    rows = LANES
    for s in range(NH):
        x_all[:, s * E : (s + 1) * E] = hot_ref[s * rows : (s + 1) * rows, :]
    for s in range(NC):
        x_all[:, (NH + s) * E : (NH + s + 1) * E] = cold[s * rows : (s + 1) * rows, :].astype(BF)
    for copy in copies[:n_copies]:
        copy.wait()
    hidden = lax.dot_general(x_all[...], down[...], NT, preferred_element_type=F32).astype(BF)
    for copy in copies[n_copies:]:
        copy.wait()
    wide = 2 * E
    chunks = [pl.ds(c * wide, wide) for c in range(F // wide)]
    logit = jnp.zeros((rows, wide), F32)
    for c in chunks:
        u = jnp.dot(hidden, up[:, c], preferred_element_type=F32) + bias_ref[c][None, :]
        upper[:, c] = u
        x = x_all[:, c].astype(F32)
        logit = logit + (x * u + x) * weight_ref[c][None, :]
    logit = jnp.sum(logit, axis=1, keepdims=True)
    at = lax.broadcasted_iota(jnp.int32, (rows, rows), 0)
    to = lax.broadcasted_iota(jnp.int32, (rows, rows), 1)
    label = jnp.sum(jnp.where(at == to, label_ref[...].astype(F32), 0.0), axis=1, keepdims=True)
    delta = 1.0 / (1.0 + jnp.exp(-logit)) - label
    for c in chunks:
        du_all[:, c] = (delta * weight_ref[c][None, :] * x_all[:, c].astype(F32)).astype(BF)
    dh = lax.dot_general(du_all[...], up[...], NT, preferred_element_type=F32).astype(BF)
    back[...] = jnp.zeros_like(back)
    for i, c in enumerate(chunks):
        grad = delta * weight_ref[c][None, :] * (upper[:, c] + 1.0) + jnp.dot(
            dh, down[:, c], preferred_element_type=F32
        )
        for j in range(2):
            s = 2 * i + j
            piece = grad[:, j * E : (j + 1) * E]
            if s < NH:
                first = piece.astype(BF)
                hot_grad[s * rows : (s + 1) * rows, :E] = first
                hot_grad[s * rows : (s + 1) * rows, E:] = (piece - first.astype(F32)).astype(BF)
            else:
                start = (s - NH) * rows
                cold[start : start + rows, :] = piece
                for k in range(start, start + rows):
                    back[pl.ds(place_ref[k], 1), :] = cold[pl.ds(k, 1), :]
    send_ref[...] = back[...].astype(BF)
    half = HOT // 2
    for core, out_ref in ((1 - core_ref[0], hot_other_ref), (core_ref[0], hot_mine_ref)):
        rows_of = pl.ds(pl.multiple_of(core * half, half), half)
        both = jnp.dot(hits[rows_of, :], hot_grad[...], preferred_element_type=F32)
        out_ref[...] = both[:, :E] + both[:, E:]


def cold_sum_body(n_data, capacity, first_ref, ask_ref, grad_ref, out_ref, hits):
    owned = out_ref.shape[0]
    blocks = ask_ref.shape[0] // n_data
    lines = []
    for d in range(n_data):
        for b in range(blocks):
            wide = min(LANES, capacity - b * LANES)
            lines.append(ask_ref[d * blocks + b : d * blocks + b + 1, :wide])
    ids = jnp.concatenate(lines, axis=1)
    names = lax.broadcasted_iota(jnp.int32, (owned, LANES), 0) + first_ref[0]
    for start in range(0, n_data * capacity, LANES):
        hits[:, start : start + LANES] = (
            (names == ids[:, start : start + LANES]).astype(F32).astype(BF)
        )
    out_ref[...] = jnp.dot(hits[...], grad_ref[...], preferred_element_type=F32)


def small_step(
    hot_ids, cold_rows, cold_owner, labels, hot_table, cold_table, cross_down, cross_up, cross_bias, out_weight
):
    rows = hot_ids.shape[0]
    n_data = lax.axis_size("dp")
    lookups = rows * NC
    capacity = 2 * ((lookups + n_data - 1) // n_data)
    owned = cold_table.shape[0]
    blocks = (capacity + LANES) // LANES
    places = n_data * capacity
    shape = jax.ShapeDtypeStruct
    owner_t = cold_owner.reshape(rows, NC).T
    place, ask = call(
        functools.partial(route_body, n_data, capacity),
        (shape((16, LANES), jnp.int32), shape((n_data * blocks, LANES), jnp.int32)),
        [VMEM, VMEM],
        [],
        (1, 1),
        "route",
    )(owner_t, cold_rows.T)
    asked = lax.all_to_all(ask, "dp", split_axis=0, concat_axis=0, tiled=True)
    hot_t = hot_ids.T
    place = place.reshape(-1)
    hot_rows = call(
        hot_rows_body,
        shape((NH * rows, E), BF),
        [SMEM, VMEM],
        [pltpu.VMEM((NH * rows, E), F32)],
        (1, 1),
        "hot_rows",
    )(hot_t.reshape(-1), hot_table)
    plane, z = weight_starts(cross_down.T, cross_up)
    asked = after(asked, hot_rows, *plane)
    z = jnp.concatenate(lax.optimization_barrier((*z, asked))[:-1], axis=1)
    found = call(
        functools.partial(serve_body, n_data, capacity),
        shape((places, E), BF),
        [SMEM, VMEM],
        [pltpu.VMEM((places, E), F32)],
        (1, 1),
        "serve",
    )(asked.reshape(-1), cold_table)
    returned = lax.all_to_all(found, "dp", split_axis=0, concat_axis=0, tiled=True)
    whole, (down_rest, up_rest) = weight_pieces(plane, z)
    pieces = [*whole, *down_rest, *up_rest]
    n_shards = sum(p.shape[-3] for p in (*whole, *down_rest))
    depth = cross_up.shape[0]
    rank = n_shards * depth
    core = lax.axis_index("rep") % 2
    send, hot_other, hot_mine = call(
        cross_body,
        (shape((places, E), BF), shape((HOT // 2, E), F32), shape((HOT // 2, E), F32)),
        [SMEM, SMEM] + [VMEM] * 6 + [ANY] * len(pieces),
        [
            pltpu.VMEM((n_shards, depth, F), BF),
            pltpu.VMEM((n_shards, depth, F), BF),
            pltpu.VMEM((places, E), F32),
            pltpu.VMEM((NC * rows, E), F32),
            pltpu.VMEM((rows, F), F32),
            pltpu.VMEM((rows, F), BF),
            pltpu.VMEM((rows, F), BF),
            pltpu.VMEM((HOT, NH * rows), BF),
            pltpu.VMEM((NH * rows, 2 * E), BF),
            pltpu.SemaphoreType.DMA((2, len(whole) + len(down_rest))),
        ],
        (8 * rows * F * rank, 20 * 10**6),
        "cross",
        58,
    )(
        core.reshape(1),
        place,
        hot_t,
        returned,
        hot_rows,
        labels.reshape(1, rows),
        cross_bias,
        out_weight,
        *pieces,
    )
    incoming = lax.all_to_all(send, "dp", split_axis=0, concat_axis=0, tiled=True)
    hot_share = hot_early(hot_mine, hot_other)
    incoming, hot_share = lax.optimization_barrier((incoming, hot_share))

    def cold_sum(rows_of, grads):
        return call(
            functools.partial(cold_sum_body, n_data, capacity),
            shape((owned // 2, E), F32),
            [SMEM, VMEM, VMEM],
            [pltpu.VMEM((owned // 2, places), BF)],
            (10**9, 10**7),
            "cold_sum",
        )((rows_of * (owned // 2)).reshape(1), asked, grads)

    others = cold_sum(1 - core, incoming)
    incoming = after(incoming, others)
    mine = cold_sum(core, incoming)
    hot_share = paired(hot_share, swap(hot_share, "dp", 1), lax.axis_index("dp") % 2)
    mine = (mine + swap(others, "rep", 1)).astype(BF)
    mine = mine.astype(F32) + swap(mine, "rep", 2).astype(F32)
    hot_share = paired(hot_share, swap(hot_share, "rep", 2), lax.axis_index("rep") // 2)
    return tuple(paired(half, swap(half, "rep", 1), core) for half in (hot_share, mine))


def large_step(
    hot_ids, cold_rows, cold_owner, labels, hot_table, cold_table, cross_down, cross_up, cross_bias, out_weight
):
    rows = hot_ids.shape[0]
    n_data = lax.axis_size("dp")
    lookups = rows * NC
    capacity = 2 * ((lookups + n_data - 1) // n_data)
    owned = cold_table.shape[0]
    owner = cold_owner.reshape(lookups)
    local_row = cold_rows.reshape(lookups)
    onehot = (owner[:, None] == jnp.arange(n_data, dtype=jnp.int32)[None, :]).astype(jnp.int32)
    running = jnp.cumsum(onehot, axis=0)
    slot = jnp.sum(onehot * running, axis=1) - 1
    place = owner * capacity + slot
    requests = (
        jnp.full((n_data * capacity,), -1, jnp.int32)
        .at[place]
        .set(local_row)
        .reshape(n_data, capacity)
    )
    asked = lax.all_to_all(requests, "dp", split_axis=0, concat_axis=0, tiled=True)
    safe = jnp.maximum(asked, 0)
    found = jnp.take(cold_table, safe, axis=0).astype(jnp.bfloat16)
    found = jnp.where((asked >= 0)[:, :, None], found, jnp.zeros_like(found))
    returned = lax.all_to_all(found, "dp", split_axis=0, concat_axis=0, tiled=True)
    cold_emb = returned.reshape(n_data * capacity, E)[place].reshape(rows, NC, E)
    hot_emb = hot_table[hot_ids].astype(jnp.bfloat16)
    first = jnp.concatenate([hot_emb, cold_emb], axis=1).reshape(rows, F)
    down_full, up_full = (
        lax.all_gather(cross_down, ("dp", "rep"), axis=1, tiled=True),
        lax.all_gather(cross_up, ("dp", "rep"), axis=0, tiled=True),
    )
    hidden = jnp.dot(first, down_full, preferred_element_type=jnp.float32).astype(jnp.bfloat16)
    upper = jnp.dot(hidden, up_full, preferred_element_type=jnp.float32) + cross_bias[None, :]
    first_f = first.astype(jnp.float32)
    second = first_f * upper + first_f
    logit = jnp.sum(second * out_weight[None, :], axis=1)
    delta = jax.nn.sigmoid(logit) - labels.astype(jnp.float32)
    d_second = delta[:, None] * out_weight[None, :]
    d_upper = (d_second * first_f).astype(jnp.bfloat16)
    d_hidden = jnp.dot(d_upper, up_full.T, preferred_element_type=jnp.float32).astype(jnp.bfloat16)
    d_first = d_second * (upper + 1.0) + jnp.dot(
        d_hidden, down_full.T, preferred_element_type=jnp.float32
    )
    grads = d_first.reshape(rows, NH + NC, E)
    hot_partial = jax.ops.segment_sum(grads[:, :NH].reshape(rows * NH, E), hot_ids.reshape(-1), HOT)
    cold_low = grads[:, NH:].astype(jnp.bfloat16).reshape(lookups, E)
    outgoing = (
        jnp.zeros((n_data * capacity, E), jnp.bfloat16)
        .at[place]
        .set(cold_low)
        .reshape(n_data, capacity, E)
    )
    incoming = lax.all_to_all(outgoing, "dp", split_axis=0, concat_axis=0, tiled=True)
    flat_ids = asked.reshape(-1)
    segment = jnp.where(flat_ids >= 0, flat_ids, owned)
    cold_partial = jax.ops.segment_sum(
        incoming.reshape(n_data * capacity, E).astype(jnp.float32), segment, owned
    )
    return lax.psum(hot_partial, ("dp", "rep")), lax.psum(cold_partial, "rep")


def shards(
    hot_ids,
    cold_rows,
    cold_owner,
    labels,
    hot_table,
    hot_backup,
    cold_table,
    cold_backup,
    cross_down,
    cross_up,
    cross_bias,
    out_weight,
):
    rows = hot_ids.shape[0]
    owned = cold_table.shape[0]
    n_data = lax.axis_size("dp")
    n_reps = lax.axis_size("rep")
    step = small_step if is_small(n_data, n_reps) else large_step
    hot_grad, cold_grad = step(
        hot_ids,
        cold_rows,
        cold_owner,
        labels,
        hot_table,
        cold_table,
        cross_down,
        cross_up,
        cross_bias,
        out_weight,
    )
    batch_all = rows * n_data * n_reps
    rate_hot = 20.0 * math.sqrt(HOT / (batch_all * NH))
    rate_cold = 20.0 * math.sqrt(owned * n_data / (batch_all * NC))
    new_hot = compensate(hot_table, hot_backup, hot_grad, rate_hot)
    new_cold = compensate(cold_table, cold_backup, cold_grad, rate_cold)
    return (new_hot, new_cold)


def solution(mesh):
    placed = (
        P(("dp", "rep"), None),
        P(("dp", "rep"), None),
        P(("dp", "rep"), None),
        P(("dp", "rep")),
        P(),
        P(),
        P("dp", None),
        P("dp", None),
        P(None, ("dp", "rep")),
        P(("dp", "rep"), None),
        P(),
        P(),
    )
    return jax.shard_map(
        shards, mesh=mesh, in_specs=placed, out_specs=(P(), P("dp", None)), check_vma=False
    )
```

```python
import functools
import math

import jax
import jax.numpy as jnp
from jax import lax
from jax.experimental import pallas as pl
from jax.experimental.pallas import tpu as pltpu
from jax.sharding import PartitionSpec as P

E = 128
NH = 13
NC = 13
HOT = 1024
F = 3328


def compensate(table, backup, grad, rate):
    step_size = rate * grad
    return table - step_size - 0.5 * step_size * step_size * (table - backup.astype(jnp.float32))


def is_small(n_data, n_reps):
    return n_reps == 4 and n_data == 8


def swap(value, axis, distance):
    size = lax.axis_size(axis)
    return lax.ppermute(value, axis, [(i, i ^ distance) for i in range(size)])


def shift(value, axis, distance):
    size = lax.axis_size(axis)
    return lax.ppermute(value, axis, [(i, (i + distance) % size) for i in range(size)])


def after(value, *others):
    return lax.optimization_barrier((value, *others))[0]


def swap_both(value):
    n_data, n_reps = lax.axis_size("dp"), lax.axis_size("rep")
    ways = [
        (d * n_reps + r, (d ^ 1) * n_reps + (r ^ 2)) for d in range(n_data) for r in range(n_reps)
    ]
    return lax.ppermute(value, ("dp", "rep"), ways)


def weight_starts(down_t, up):
    own = jnp.stack([down_t, up])[:, None]
    z = [swap(own, "dp", 2 * k) for k in range(1, lax.axis_size("dp") // 2)]
    over_x, over_y = swap(own, "rep", 2), swap(own, "dp", 1)
    return [own, over_x, over_y, swap_both(own)], z


def weight_pieces(plane, z):
    over_x, over_y = swap(z, "rep", 2), swap(z, "dp", 1)
    across = swap(over_y[0], "rep", 2), swap(over_x[1], "dp", 1)
    whole = [*plane, z, over_x, over_y]
    whole += [swap(piece, "rep", 1) for piece in whole]
    return whole, [(piece, swap(piece, "rep", 1)) for piece in across]


def half_of(value, index, count):
    rows = value.shape[0] // count
    return lax.dynamic_slice_in_dim(value, index * rows, rows, axis=0)


def paired(mine, other, index):
    return jnp.where(
        index == 0,
        jnp.concatenate([mine, other], axis=0),
        jnp.concatenate([other, mine], axis=0),
    )


def hot_early(mine, other):
    total = mine + swap(other, "rep", 1)
    for axis, distance, index in (
        ("rep", 2, lax.axis_index("rep") // 2),
        ("dp", 1, lax.axis_index("dp") % 2),
    ):
        total = half_of(total, index, 2) + swap(half_of(total, 1 - index, 2), axis, distance)
    for distance in (2, 4):
        total = total + swap(total, "dp", distance)
    return total


LANES = 128
GROUP = 32
BF = jnp.bfloat16
F32 = jnp.float32
VMEM = pl.BlockSpec(memory_space=pltpu.VMEM)
SMEM = pl.BlockSpec(memory_space=pltpu.SMEM)
ANY = pl.BlockSpec(memory_space=pl.ANY)
NT = (((1,), (1,)), ((), ()))


def call(body, out_shape, in_specs, scratch, cost, name, limit=40):
    flops, moved = cost
    single = not isinstance(out_shape, tuple)
    return pl.pallas_call(
        body,
        out_shape=out_shape,
        in_specs=in_specs,
        out_specs=VMEM if single else tuple([VMEM] * len(out_shape)),
        scratch_shapes=scratch,
        compiler_params=pltpu.CompilerParams(vmem_limit_bytes=limit << 20),
        cost_estimate=pl.CostEstimate(flops=flops, bytes_accessed=moved, transcendentals=0),
        name=name,
    )


def route_body(n_data, capacity, owner_ref, row_ref, place_ref, ask_ref):
    lines = owner_ref.shape[0]
    padded = place_ref.shape[0]
    blocks = ask_ref.shape[0] // n_data
    count = n_data * padded
    owner = jnp.concatenate(
        [owner_ref[...], jnp.full((padded - lines, LANES), -1, jnp.int32)], axis=0
    )
    named = jnp.concatenate([(owner == d).astype(F32) for d in range(n_data)], axis=0).astype(BF)
    at = lax.broadcasted_iota(jnp.int32, (LANES, LANES), 0)
    to = lax.broadcasted_iota(jnp.int32, (LANES, LANES), 1)
    before = (at < to).astype(F32).astype(BF)
    within = jnp.dot(named, before, preferred_element_type=F32)
    sums = jnp.dot(named, jnp.ones((LANES, LANES), BF), preferred_element_type=F32)
    line = lax.broadcasted_iota(jnp.int32, (count, count), 0)
    other = lax.broadcasted_iota(jnp.int32, (count, count), 1)
    above = ((line // padded == other // padded) & (other < line)).astype(F32).astype(BF)
    rank = within + jnp.dot(above, sums.astype(BF), preferred_element_type=F32)
    slot = jnp.zeros((padded, LANES), F32)
    for d in range(n_data):
        slot = slot + jnp.where(owner == d, rank[d * padded : (d + 1) * padded], 0.0)
    slot = slot.astype(jnp.int32)
    place_ref[...] = owner * capacity + slot
    high = owner * blocks + slot // LANES
    low = slot % LANES
    asks = ask_ref.shape[0]
    ask_line = lax.broadcasted_iota(jnp.int32, (asks, LANES), 0)
    lefts, rights = [], []
    for s in range(lines):
        hit = ask_line == high[s : s + 1]
        row = row_ref[s : s + 1]
        zero = jnp.zeros((asks, LANES), F32)
        lefts.append(
            jnp.concatenate(
                [
                    jnp.where(hit, (row // 16).astype(F32), zero),
                    jnp.where(hit, (row % 16).astype(F32), zero),
                ],
                axis=0,
            ).astype(BF)
        )
        rights.append((at == low[s : s + 1]).astype(F32).astype(BF))
    found = lax.dot_general(
        jnp.concatenate(lefts, axis=1),
        jnp.concatenate(rights, axis=1),
        NT,
        preferred_element_type=F32,
    )
    asked = found[:asks] * 16.0 + found[asks:]
    lane = lax.broadcasted_iota(jnp.int32, (asks, LANES), 1)
    for d in range(n_data):
        total = jnp.sum(sums[d * padded : (d + 1) * padded], axis=0, keepdims=True)
        asked = jnp.where((ask_line == d * blocks + blocks - 1) & (lane == LANES - 1), total, asked)
    ask_ref[...] = asked.astype(jnp.int32)


def serve_body(n_data, capacity, ask_ref, table_ref, out_ref, found):
    block = ask_ref.shape[0] // n_data
    found[...] = jnp.zeros_like(found)
    for d in range(n_data):

        def group(g, carry, d=d):
            start = pl.multiple_of(d * capacity + g * GROUP, GROUP)
            rows = [ask_ref[d * block + g * GROUP + k] for k in range(GROUP)]
            taken = [table_ref[pl.ds(row, 1), :] for row in rows]
            for k in range(GROUP):
                found[pl.ds(start + k, 1), :] = taken[k]
            return carry

        asked = ask_ref[(d + 1) * block - 1]
        lax.fori_loop(0, (asked + GROUP - 1) // GROUP, group, 0)
    out_ref[...] = found[...].astype(BF)


def pick(index_ref, source, into):
    def group(g, carry):
        start = pl.multiple_of(g * GROUP, GROUP)
        rows = [index_ref[start + k] for k in range(GROUP)]
        taken = [source[pl.ds(row, 1), :] for row in rows]
        for k in range(GROUP):
            into[pl.ds(start + k, 1), :] = taken[k]
        return carry

    lax.fori_loop(0, into.shape[0] // GROUP, group, 0)


def hot_rows_body(id_ref, table_ref, out_ref, found):
    pick(id_ref, table_ref, found)
    out_ref[...] = found[...].astype(BF)


def cross_body(
    core_ref,
    place_ref,
    id_ref,
    back_ref,
    hot_ref,
    label_ref,
    bias_ref,
    weight_ref,
    *rest,
):
    n_pieces = len(rest) - 13
    pieces = rest[:n_pieces]
    send_ref, hot_other_ref, hot_mine_ref, *scratch = rest[n_pieces:]
    downs, ups, back, cold, upper, x_all, du_all, hits, hot_grad, sem = scratch
    copies = []
    whole = [piece for piece in pieces if len(piece.shape) == 4]
    parts = [piece for piece in pieces if len(piece.shape) == 3]
    n_parts = len(parts) // 2
    for part, target in ((0, downs), (1, ups)):
        sources = [piece.at[part] for piece in whole]
        sources += parts[part * n_parts : (part + 1) * n_parts]
        first = 0
        for i, source in enumerate(sources):
            count = source.shape[0]
            copy = pltpu.make_async_copy(source, target.at[pl.ds(first, count)], sem.at[part, i])
            copy.start()
            copies.append(copy)
            first += count
    n_copies = len(copies) // 2
    down = downs.reshape(downs.shape[0] * downs.shape[1], F)
    up = ups.reshape(ups.shape[0] * ups.shape[1], F)
    names = lax.broadcasted_iota(jnp.int32, (HOT, LANES), 0)
    for s in range(NH):
        hits[:, s * LANES : (s + 1) * LANES] = (names == id_ref[s : s + 1, :]).astype(F32).astype(BF)
    back[...] = back_ref[...].astype(F32)
    pick(place_ref, back, cold)
    rows = LANES
    for s in range(NH):
        x_all[:, s * E : (s + 1) * E] = hot_ref[s * rows : (s + 1) * rows, :]
    for s in range(NC):
        x_all[:, (NH + s) * E : (NH + s + 1) * E] = cold[s * rows : (s + 1) * rows, :].astype(BF)
    for copy in copies[:n_copies]:
        copy.wait()
    hidden = lax.dot_general(x_all[...], down[...], NT, preferred_element_type=F32).astype(BF)
    for copy in copies[n_copies:]:
        copy.wait()
    wide = 2 * E
    chunks = [pl.ds(c * wide, wide) for c in range(F // wide)]
    logit = jnp.zeros((rows, wide), F32)
    for c in chunks:
        u = jnp.dot(hidden, up[:, c], preferred_element_type=F32) + bias_ref[c][None, :]
        upper[:, c] = u
        x = x_all[:, c].astype(F32)
        logit = logit + (x * u + x) * weight_ref[c][None, :]
    logit = jnp.sum(logit, axis=1, keepdims=True)
    at = lax.broadcasted_iota(jnp.int32, (rows, rows), 0)
    to = lax.broadcasted_iota(jnp.int32, (rows, rows), 1)
    label = jnp.sum(jnp.where(at == to, label_ref[...].astype(F32), 0.0), axis=1, keepdims=True)
    delta = 1.0 / (1.0 + jnp.exp(-logit)) - label
    for c in chunks:
        du_all[:, c] = (delta * weight_ref[c][None, :] * x_all[:, c].astype(F32)).astype(BF)
    dh = lax.dot_general(du_all[...], up[...], NT, preferred_element_type=F32).astype(BF)
    back[...] = jnp.zeros_like(back)
    for i, c in enumerate(chunks):
        grad = delta * weight_ref[c][None, :] * (upper[:, c] + 1.0) + jnp.dot(
            dh, down[:, c], preferred_element_type=F32
        )
        for j in range(2):
            s = 2 * i + j
            piece = grad[:, j * E : (j + 1) * E]
            if s < NH:
                first = piece.astype(BF)
                hot_grad[s * rows : (s + 1) * rows, :E] = first
                hot_grad[s * rows : (s + 1) * rows, E:] = (piece - first.astype(F32)).astype(BF)
            else:
                start = (s - NH) * rows
                cold[start : start + rows, :] = piece
                for k in range(start, start + rows):
                    back[pl.ds(place_ref[k], 1), :] = cold[pl.ds(k, 1), :]
    send_ref[...] = back[...].astype(BF)
    half = HOT // 2
    for core, out_ref in ((1 - core_ref[0], hot_other_ref), (core_ref[0], hot_mine_ref)):
        rows_of = pl.ds(pl.multiple_of(core * half, half), half)
        both = jnp.dot(hits[rows_of, :], hot_grad[...], preferred_element_type=F32)
        out_ref[...] = both[:, :E] + both[:, E:]


def cold_sum_body(n_data, capacity, first_ref, ask_ref, grad_ref, out_ref, hits):
    owned = out_ref.shape[0]
    blocks = ask_ref.shape[0] // n_data
    lines = []
    for d in range(n_data):
        for b in range(blocks):
            wide = min(LANES, capacity - b * LANES)
            lines.append(ask_ref[d * blocks + b : d * blocks + b + 1, :wide])
    ids = jnp.concatenate(lines, axis=1)
    names = lax.broadcasted_iota(jnp.int32, (owned, LANES), 0) + first_ref[0]
    for start in range(0, n_data * capacity, LANES):
        hits[:, start : start + LANES] = (
            (names == ids[:, start : start + LANES]).astype(F32).astype(BF)
        )
    out_ref[...] = jnp.dot(hits[...], grad_ref[...], preferred_element_type=F32)


def small_step(
    hot_ids, cold_rows, cold_owner, labels, hot_table, cold_table, cross_down, cross_up, cross_bias, out_weight
):
    rows = hot_ids.shape[0]
    n_data = lax.axis_size("dp")
    lookups = rows * NC
    capacity = 2 * ((lookups + n_data - 1) // n_data)
    owned = cold_table.shape[0]
    blocks = (capacity + LANES) // LANES
    places = n_data * capacity
    shape = jax.ShapeDtypeStruct
    owner_t = cold_owner.reshape(rows, NC).T
    place, ask = call(
        functools.partial(route_body, n_data, capacity),
        (shape((16, LANES), jnp.int32), shape((n_data * blocks, LANES), jnp.int32)),
        [VMEM, VMEM],
        [],
        (1, 1),
        "route",
    )(owner_t, cold_rows.T)
    asked = lax.all_to_all(ask, "dp", split_axis=0, concat_axis=0, tiled=True)
    hot_t = hot_ids.T
    place = place.reshape(-1)
    hot_rows = call(
        hot_rows_body,
        shape((NH * rows, E), BF),
        [SMEM, VMEM],
        [pltpu.VMEM((NH * rows, E), F32)],
        (1, 1),
        "hot_rows",
    )(hot_t.reshape(-1), hot_table)
    plane, z = weight_starts(cross_down.T, cross_up)
    z = jnp.concatenate(z, axis=1)
    asked, z = lax.optimization_barrier((asked, z, hot_rows, *plane))[:2]
    found = call(
        functools.partial(serve_body, n_data, capacity),
        shape((places, E), BF),
        [SMEM, VMEM],
        [pltpu.VMEM((places, E), F32)],
        (1, 1),
        "serve",
    )(asked.reshape(-1), cold_table)
    returned = lax.all_to_all(found, "dp", split_axis=0, concat_axis=0, tiled=True)
    whole, (down_rest, up_rest) = weight_pieces(plane, z)
    pieces = [*whole, *down_rest, *up_rest]
    n_shards = sum(p.shape[-3] for p in (*whole, *down_rest))
    depth = cross_up.shape[0]
    rank = n_shards * depth
    core = lax.axis_index("rep") % 2
    send, hot_other, hot_mine = call(
        cross_body,
        (shape((places, E), BF), shape((HOT // 2, E), F32), shape((HOT // 2, E), F32)),
        [SMEM, SMEM] + [VMEM] * 6 + [ANY] * len(pieces),
        [
            pltpu.VMEM((n_shards, depth, F), BF),
            pltpu.VMEM((n_shards, depth, F), BF),
            pltpu.VMEM((places, E), F32),
            pltpu.VMEM((NC * rows, E), F32),
            pltpu.VMEM((rows, F), F32),
            pltpu.VMEM((rows, F), BF),
            pltpu.VMEM((rows, F), BF),
            pltpu.VMEM((HOT, NH * rows), BF),
            pltpu.VMEM((NH * rows, 2 * E), BF),
            pltpu.SemaphoreType.DMA((2, len(whole) + len(down_rest))),
        ],
        (8 * rows * F * rank, 20 * 10**6),
        "cross",
        58,
    )(
        core.reshape(1),
        place,
        hot_t,
        returned,
        hot_rows,
        labels.reshape(1, rows),
        cross_bias,
        out_weight,
        *pieces,
    )
    incoming = lax.all_to_all(send, "dp", split_axis=0, concat_axis=0, tiled=True)
    hot_share = hot_early(hot_mine, hot_other)
    incoming, hot_share = lax.optimization_barrier((incoming, hot_share))

    def cold_sum(rows_of, grads):
        return call(
            functools.partial(cold_sum_body, n_data, capacity),
            shape((owned // 2, E), F32),
            [SMEM, VMEM, VMEM],
            [pltpu.VMEM((owned // 2, places), BF)],
            (10**9, 10**7),
            "cold_sum",
        )((rows_of * (owned // 2)).reshape(1), asked, grads)

    others = cold_sum(1 - core, incoming)
    incoming = after(incoming, others)
    mine = cold_sum(core, incoming)
    hot_share = paired(hot_share, swap(hot_share, "dp", 1), lax.axis_index("dp") % 2)
    mine = (mine + swap(others, "rep", 1)).astype(BF)
    mine = mine.astype(F32) + swap(mine, "rep", 2).astype(F32)
    hot_share = paired(hot_share, swap(hot_share, "rep", 2), lax.axis_index("rep") // 2)
    return tuple(paired(half, swap(half, "rep", 1), core) for half in (hot_share, mine))


def large_step(
    hot_ids, cold_rows, cold_owner, labels, hot_table, cold_table, cross_down, cross_up, cross_bias, out_weight
):
    rows = hot_ids.shape[0]
    n_data = lax.axis_size("dp")
    lookups = rows * NC
    capacity = 2 * ((lookups + n_data - 1) // n_data)
    owned = cold_table.shape[0]
    owner = cold_owner.reshape(lookups)
    local_row = cold_rows.reshape(lookups)
    onehot = (owner[:, None] == jnp.arange(n_data, dtype=jnp.int32)[None, :]).astype(jnp.int32)
    running = jnp.cumsum(onehot, axis=0)
    slot = jnp.sum(onehot * running, axis=1) - 1
    place = owner * capacity + slot
    requests = (
        jnp.full((n_data * capacity,), -1, jnp.int32)
        .at[place]
        .set(local_row)
        .reshape(n_data, capacity)
    )
    asked = lax.all_to_all(requests, "dp", split_axis=0, concat_axis=0, tiled=True)
    safe = jnp.maximum(asked, 0)
    found = jnp.take(cold_table, safe, axis=0).astype(jnp.bfloat16)
    found = jnp.where((asked >= 0)[:, :, None], found, jnp.zeros_like(found))
    returned = lax.all_to_all(found, "dp", split_axis=0, concat_axis=0, tiled=True)
    cold_emb = returned.reshape(n_data * capacity, E)[place].reshape(rows, NC, E)
    hot_emb = hot_table[hot_ids].astype(jnp.bfloat16)
    first = jnp.concatenate([hot_emb, cold_emb], axis=1).reshape(rows, F)
    down_full, up_full = (
        lax.all_gather(cross_down, ("dp", "rep"), axis=1, tiled=True),
        lax.all_gather(cross_up, ("dp", "rep"), axis=0, tiled=True),
    )
    hidden = jnp.dot(first, down_full, preferred_element_type=jnp.float32).astype(jnp.bfloat16)
    upper = jnp.dot(hidden, up_full, preferred_element_type=jnp.float32) + cross_bias[None, :]
    first_f = first.astype(jnp.float32)
    second = first_f * upper + first_f
    logit = jnp.sum(second * out_weight[None, :], axis=1)
    delta = jax.nn.sigmoid(logit) - labels.astype(jnp.float32)
    d_second = delta[:, None] * out_weight[None, :]
    d_upper = (d_second * first_f).astype(jnp.bfloat16)
    d_hidden = jnp.dot(d_upper, up_full.T, preferred_element_type=jnp.float32).astype(jnp.bfloat16)
    d_first = d_second * (upper + 1.0) + jnp.dot(
        d_hidden, down_full.T, preferred_element_type=jnp.float32
    )
    grads = d_first.reshape(rows, NH + NC, E)
    hot_partial = jax.ops.segment_sum(grads[:, :NH].reshape(rows * NH, E), hot_ids.reshape(-1), HOT)
    cold_low = grads[:, NH:].astype(jnp.bfloat16).reshape(lookups, E)
    outgoing = (
        jnp.zeros((n_data * capacity, E), jnp.bfloat16)
        .at[place]
        .set(cold_low)
        .reshape(n_data, capacity, E)
    )
    incoming = lax.all_to_all(outgoing, "dp", split_axis=0, concat_axis=0, tiled=True)
    flat_ids = asked.reshape(-1)
    segment = jnp.where(flat_ids >= 0, flat_ids, owned)
    cold_partial = jax.ops.segment_sum(
        incoming.reshape(n_data * capacity, E).astype(jnp.float32), segment, owned
    )
    return lax.psum(hot_partial, ("dp", "rep")), lax.psum(cold_partial, "rep")


def shards(
    hot_ids,
    cold_rows,
    cold_owner,
    labels,
    hot_table,
    hot_backup,
    cold_table,
    cold_backup,
    cross_down,
    cross_up,
    cross_bias,
    out_weight,
):
    rows = hot_ids.shape[0]
    owned = cold_table.shape[0]
    n_data = lax.axis_size("dp")
    n_reps = lax.axis_size("rep")
    step = small_step if is_small(n_data, n_reps) else large_step
    hot_grad, cold_grad = step(
        hot_ids,
        cold_rows,
        cold_owner,
        labels,
        hot_table,
        cold_table,
        cross_down,
        cross_up,
        cross_bias,
        out_weight,
    )
    batch_all = rows * n_data * n_reps
    rate_hot = 20.0 * math.sqrt(HOT / (batch_all * NH))
    rate_cold = 20.0 * math.sqrt(owned * n_data / (batch_all * NC))
    new_hot = compensate(hot_table, hot_backup, hot_grad, rate_hot)
    new_cold = compensate(cold_table, cold_backup, cold_grad, rate_cold)
    return (new_hot, new_cold)


def solution(mesh):
    placed = (
        P(("dp", "rep"), None),
        P(("dp", "rep"), None),
        P(("dp", "rep"), None),
        P(("dp", "rep")),
        P(),
        P(),
        P("dp", None),
        P("dp", None),
        P(None, ("dp", "rep")),
        P(("dp", "rep"), None),
        P(),
        P(),
    )
    return jax.shard_map(
        shards, mesh=mesh, in_specs=placed, out_specs=(P(), P("dp", None)), check_vma=False
    )
```

```python
import functools
import math

import jax
import jax.numpy as jnp
from jax import lax
from jax.experimental import pallas as pl
from jax.experimental.pallas import tpu as pltpu
from jax.sharding import PartitionSpec as P

E = 128
NH = 13
NC = 13
HOT = 1024
F = 3328


def compensate(table, backup, grad, rate):
    step_size = rate * grad
    return table - step_size - 0.5 * step_size * step_size * (table - backup.astype(jnp.float32))


def is_small(n_data, n_reps):
    return n_reps == 4 and n_data == 8


def swap(value, axis, distance):
    size = lax.axis_size(axis)
    return lax.ppermute(value, axis, [(i, i ^ distance) for i in range(size)])


def shift(value, axis, distance):
    size = lax.axis_size(axis)
    return lax.ppermute(value, axis, [(i, (i + distance) % size) for i in range(size)])


def after(value, *others):
    return lax.optimization_barrier((value, *others))[0]


def swap_both(value):
    n_data, n_reps = lax.axis_size("dp"), lax.axis_size("rep")
    ways = [
        (d * n_reps + r, (d ^ 1) * n_reps + (r ^ 2)) for d in range(n_data) for r in range(n_reps)
    ]
    return lax.ppermute(value, ("dp", "rep"), ways)


def weight_starts(down_t, up):
    own = jnp.stack([down_t, up])[:, None]
    z = [swap(own, "dp", 2 * k) for k in range(1, lax.axis_size("dp") // 2)]
    over_x, over_y = swap(own, "rep", 2), swap(own, "dp", 1)
    return [own, over_x, over_y, swap_both(own)], z


def weight_pieces(plane, z):
    over_x, over_y = swap(z, "rep", 2), swap(z, "dp", 1)
    across = swap(over_y[0], "rep", 2), swap(over_x[1], "dp", 1)
    whole = [*plane, z, over_x, over_y]
    whole += [swap(piece, "rep", 1) for piece in whole]
    return whole, [(piece, swap(piece, "rep", 1)) for piece in across]


def half_of(value, index, count):
    rows = value.shape[0] // count
    return lax.dynamic_slice_in_dim(value, index * rows, rows, axis=0)


def paired(mine, other, index):
    return jnp.where(
        index == 0,
        jnp.concatenate([mine, other], axis=0),
        jnp.concatenate([other, mine], axis=0),
    )


def hot_early(mine, other):
    total = mine + swap(other, "rep", 1)
    for axis, distance, index in (
        ("rep", 2, lax.axis_index("rep") // 2),
        ("dp", 1, lax.axis_index("dp") % 2),
    ):
        total = half_of(total, index, 2) + swap(half_of(total, 1 - index, 2), axis, distance)
    return total + swap(total, "dp", 2)


LANES = 128
GROUP = 32
BF = jnp.bfloat16
F32 = jnp.float32
VMEM = pl.BlockSpec(memory_space=pltpu.VMEM)
SMEM = pl.BlockSpec(memory_space=pltpu.SMEM)
ANY = pl.BlockSpec(memory_space=pl.ANY)
NT = (((1,), (1,)), ((), ()))


def call(body, out_shape, in_specs, scratch, cost, name, limit=40):
    flops, moved = cost
    single = not isinstance(out_shape, tuple)
    return pl.pallas_call(
        body,
        out_shape=out_shape,
        in_specs=in_specs,
        out_specs=VMEM if single else tuple([VMEM] * len(out_shape)),
        scratch_shapes=scratch,
        compiler_params=pltpu.CompilerParams(vmem_limit_bytes=limit << 20),
        cost_estimate=pl.CostEstimate(flops=flops, bytes_accessed=moved, transcendentals=0),
        name=name,
    )


def route_body(n_data, capacity, owner_ref, row_ref, place_ref, ask_ref):
    lines = owner_ref.shape[0]
    padded = place_ref.shape[0]
    blocks = ask_ref.shape[0] // n_data
    count = n_data * padded
    owner = jnp.concatenate(
        [owner_ref[...], jnp.full((padded - lines, LANES), -1, jnp.int32)], axis=0
    )
    named = jnp.concatenate([(owner == d).astype(F32) for d in range(n_data)], axis=0).astype(BF)
    at = lax.broadcasted_iota(jnp.int32, (LANES, LANES), 0)
    to = lax.broadcasted_iota(jnp.int32, (LANES, LANES), 1)
    before = (at < to).astype(F32).astype(BF)
    within = jnp.dot(named, before, preferred_element_type=F32)
    sums = jnp.dot(named, jnp.ones((LANES, LANES), BF), preferred_element_type=F32)
    line = lax.broadcasted_iota(jnp.int32, (count, count), 0)
    other = lax.broadcasted_iota(jnp.int32, (count, count), 1)
    above = ((line // padded == other // padded) & (other < line)).astype(F32).astype(BF)
    rank = within + jnp.dot(above, sums.astype(BF), preferred_element_type=F32)
    slot = jnp.zeros((padded, LANES), F32)
    for d in range(n_data):
        slot = slot + jnp.where(owner == d, rank[d * padded : (d + 1) * padded], 0.0)
    slot = slot.astype(jnp.int32)
    place_ref[...] = owner * capacity + slot
    high = owner * blocks + slot // LANES
    low = slot % LANES
    asks = ask_ref.shape[0]
    ask_line = lax.broadcasted_iota(jnp.int32, (asks, LANES), 0)
    lefts, rights = [], []
    for s in range(lines):
        hit = ask_line == high[s : s + 1]
        row = row_ref[s : s + 1]
        zero = jnp.zeros((asks, LANES), F32)
        lefts.append(
            jnp.concatenate(
                [
                    jnp.where(hit, (row // 16).astype(F32), zero),
                    jnp.where(hit, (row % 16).astype(F32), zero),
                ],
                axis=0,
            ).astype(BF)
        )
        rights.append((at == low[s : s + 1]).astype(F32).astype(BF))
    found = lax.dot_general(
        jnp.concatenate(lefts, axis=1),
        jnp.concatenate(rights, axis=1),
        NT,
        preferred_element_type=F32,
    )
    asked = found[:asks] * 16.0 + found[asks:]
    lane = lax.broadcasted_iota(jnp.int32, (asks, LANES), 1)
    for d in range(n_data):
        total = jnp.sum(sums[d * padded : (d + 1) * padded], axis=0, keepdims=True)
        asked = jnp.where((ask_line == d * blocks + blocks - 1) & (lane == LANES - 1), total, asked)
    ask_ref[...] = asked.astype(jnp.int32)


def serve_body(n_data, capacity, ask_ref, table_ref, out_ref, found):
    block = ask_ref.shape[0] // n_data
    found[...] = jnp.zeros_like(found)
    for d in range(n_data):

        def group(g, carry, d=d):
            start = pl.multiple_of(d * capacity + g * GROUP, GROUP)
            rows = [ask_ref[d * block + g * GROUP + k] for k in range(GROUP)]
            taken = [table_ref[pl.ds(row, 1), :] for row in rows]
            for k in range(GROUP):
                found[pl.ds(start + k, 1), :] = taken[k]
            return carry

        asked = ask_ref[(d + 1) * block - 1]
        lax.fori_loop(0, (asked + GROUP - 1) // GROUP, group, 0)
    out_ref[...] = found[...].astype(BF)


def pick(index_ref, source, into):
    def group(g, carry):
        start = pl.multiple_of(g * GROUP, GROUP)
        rows = [index_ref[start + k] for k in range(GROUP)]
        taken = [source[pl.ds(row, 1), :] for row in rows]
        for k in range(GROUP):
            into[pl.ds(start + k, 1), :] = taken[k]
        return carry

    lax.fori_loop(0, into.shape[0] // GROUP, group, 0)


def hot_rows_body(id_ref, table_ref, out_ref, found):
    pick(id_ref, table_ref, found)
    out_ref[...] = found[...].astype(BF)


def cross_body(
    core_ref,
    place_ref,
    id_ref,
    back_ref,
    hot_ref,
    label_ref,
    bias_ref,
    weight_ref,
    *rest,
):
    n_pieces = len(rest) - 13
    pieces = rest[:n_pieces]
    send_ref, hot_other_ref, hot_mine_ref, *scratch = rest[n_pieces:]
    downs, ups, back, cold, upper, x_all, du_all, hits, hot_grad, sem = scratch
    copies = []
    whole = [piece for piece in pieces if len(piece.shape) == 4]
    parts = [piece for piece in pieces if len(piece.shape) == 3]
    n_parts = len(parts) // 2
    for part, target in ((0, downs), (1, ups)):
        sources = [piece.at[part] for piece in whole]
        sources += parts[part * n_parts : (part + 1) * n_parts]
        first = 0
        for i, source in enumerate(sources):
            count = source.shape[0]
            copy = pltpu.make_async_copy(source, target.at[pl.ds(first, count)], sem.at[part, i])
            copy.start()
            copies.append(copy)
            first += count
    n_copies = len(copies) // 2
    down = downs.reshape(downs.shape[0] * downs.shape[1], F)
    up = ups.reshape(ups.shape[0] * ups.shape[1], F)
    names = lax.broadcasted_iota(jnp.int32, (HOT, LANES), 0)
    for s in range(NH):
        hits[:, s * LANES : (s + 1) * LANES] = (names == id_ref[s : s + 1, :]).astype(F32).astype(BF)
    back[...] = back_ref[...].astype(F32)
    pick(place_ref, back, cold)
    rows = LANES
    for s in range(NH):
        x_all[:, s * E : (s + 1) * E] = hot_ref[s * rows : (s + 1) * rows, :]
    for s in range(NC):
        x_all[:, (NH + s) * E : (NH + s + 1) * E] = cold[s * rows : (s + 1) * rows, :].astype(BF)
    for copy in copies[:n_copies]:
        copy.wait()
    hidden = lax.dot_general(x_all[...], down[...], NT, preferred_element_type=F32).astype(BF)
    for copy in copies[n_copies:]:
        copy.wait()
    wide = 2 * E
    chunks = [pl.ds(c * wide, wide) for c in range(F // wide)]
    logit = jnp.zeros((rows, wide), F32)
    for c in chunks:
        u = jnp.dot(hidden, up[:, c], preferred_element_type=F32) + bias_ref[c][None, :]
        upper[:, c] = u
        x = x_all[:, c].astype(F32)
        logit = logit + (x * u + x) * weight_ref[c][None, :]
    logit = jnp.sum(logit, axis=1, keepdims=True)
    at = lax.broadcasted_iota(jnp.int32, (rows, rows), 0)
    to = lax.broadcasted_iota(jnp.int32, (rows, rows), 1)
    label = jnp.sum(jnp.where(at == to, label_ref[...].astype(F32), 0.0), axis=1, keepdims=True)
    delta = 1.0 / (1.0 + jnp.exp(-logit)) - label
    for c in chunks:
        du_all[:, c] = (delta * weight_ref[c][None, :] * x_all[:, c].astype(F32)).astype(BF)
    dh = lax.dot_general(du_all[...], up[...], NT, preferred_element_type=F32).astype(BF)
    back[...] = jnp.zeros_like(back)
    for i, c in enumerate(chunks):
        grad = delta * weight_ref[c][None, :] * (upper[:, c] + 1.0) + jnp.dot(
            dh, down[:, c], preferred_element_type=F32
        )
        for j in range(2):
            s = 2 * i + j
            piece = grad[:, j * E : (j + 1) * E]
            if s < NH:
                first = piece.astype(BF)
                hot_grad[s * rows : (s + 1) * rows, :E] = first
                hot_grad[s * rows : (s + 1) * rows, E:] = (piece - first.astype(F32)).astype(BF)
            else:
                start = (s - NH) * rows
                cold[start : start + rows, :] = piece
                for k in range(start, start + rows):
                    back[pl.ds(place_ref[k], 1), :] = cold[pl.ds(k, 1), :]
    send_ref[...] = back[...].astype(BF)
    half = HOT // 2
    for core, out_ref in ((1 - core_ref[0], hot_other_ref), (core_ref[0], hot_mine_ref)):
        rows_of = pl.ds(pl.multiple_of(core * half, half), half)
        both = jnp.dot(hits[rows_of, :], hot_grad[...], preferred_element_type=F32)
        out_ref[...] = both[:, :E] + both[:, E:]


def cold_sum_body(n_data, capacity, first_ref, ask_ref, grad_ref, out_ref, hits):
    owned = out_ref.shape[0]
    blocks = ask_ref.shape[0] // n_data
    lines = []
    for d in range(n_data):
        for b in range(blocks):
            wide = min(LANES, capacity - b * LANES)
            lines.append(ask_ref[d * blocks + b : d * blocks + b + 1, :wide])
    ids = jnp.concatenate(lines, axis=1)
    names = lax.broadcasted_iota(jnp.int32, (owned, LANES), 0) + first_ref[0]
    for start in range(0, n_data * capacity, LANES):
        hits[:, start : start + LANES] = (
            (names == ids[:, start : start + LANES]).astype(F32).astype(BF)
        )
    out_ref[...] = jnp.dot(hits[...], grad_ref[...], preferred_element_type=F32)


def small_step(
    hot_ids, cold_rows, cold_owner, labels, hot_table, cold_table, cross_down, cross_up, cross_bias, out_weight
):
    rows = hot_ids.shape[0]
    n_data = lax.axis_size("dp")
    lookups = rows * NC
    capacity = 2 * ((lookups + n_data - 1) // n_data)
    owned = cold_table.shape[0]
    blocks = (capacity + LANES) // LANES
    places = n_data * capacity
    shape = jax.ShapeDtypeStruct
    owner_t = cold_owner.reshape(rows, NC).T
    place, ask = call(
        functools.partial(route_body, n_data, capacity),
        (shape((16, LANES), jnp.int32), shape((n_data * blocks, LANES), jnp.int32)),
        [VMEM, VMEM],
        [],
        (1, 1),
        "route",
    )(owner_t, cold_rows.T)
    asked = lax.all_to_all(ask, "dp", split_axis=0, concat_axis=0, tiled=True)
    hot_t = hot_ids.T
    place = place.reshape(-1)
    hot_rows = call(
        hot_rows_body,
        shape((NH * rows, E), BF),
        [SMEM, VMEM],
        [pltpu.VMEM((NH * rows, E), F32)],
        (1, 1),
        "hot_rows",
    )(hot_t.reshape(-1), hot_table)
    plane, z = weight_starts(cross_down.T, cross_up)
    z = jnp.concatenate(z, axis=1)
    asked, z = lax.optimization_barrier((asked, z, hot_rows, *plane))[:2]
    found = call(
        functools.partial(serve_body, n_data, capacity),
        shape((places, E), BF),
        [SMEM, VMEM],
        [pltpu.VMEM((places, E), F32)],
        (1, 1),
        "serve",
    )(asked.reshape(-1), cold_table)
    returned = lax.all_to_all(found, "dp", split_axis=0, concat_axis=0, tiled=True)
    whole, (down_rest, up_rest) = weight_pieces(plane, z)
    pieces = [*whole, *down_rest, *up_rest]
    n_shards = sum(p.shape[-3] for p in (*whole, *down_rest))
    depth = cross_up.shape[0]
    rank = n_shards * depth
    core = lax.axis_index("rep") % 2
    send, hot_other, hot_mine = call(
        cross_body,
        (shape((places, E), BF), shape((HOT // 2, E), F32), shape((HOT // 2, E), F32)),
        [SMEM, SMEM] + [VMEM] * 6 + [ANY] * len(pieces),
        [
            pltpu.VMEM((n_shards, depth, F), BF),
            pltpu.VMEM((n_shards, depth, F), BF),
            pltpu.VMEM((places, E), F32),
            pltpu.VMEM((NC * rows, E), F32),
            pltpu.VMEM((rows, F), F32),
            pltpu.VMEM((rows, F), BF),
            pltpu.VMEM((rows, F), BF),
            pltpu.VMEM((HOT, NH * rows), BF),
            pltpu.VMEM((NH * rows, 2 * E), BF),
            pltpu.SemaphoreType.DMA((2, len(whole) + len(down_rest))),
        ],
        (8 * rows * F * rank, 20 * 10**6),
        "cross",
        58,
    )(
        core.reshape(1),
        place,
        hot_t,
        returned,
        hot_rows,
        labels.reshape(1, rows),
        cross_bias,
        out_weight,
        *pieces,
    )
    incoming = lax.all_to_all(send, "dp", split_axis=0, concat_axis=0, tiled=True)
    hot_share = hot_early(hot_mine, hot_other)
    incoming, hot_share = lax.optimization_barrier((incoming, hot_share))

    def cold_sum(rows_of, grads):
        return call(
            functools.partial(cold_sum_body, n_data, capacity),
            shape((owned // 2, E), F32),
            [SMEM, VMEM, VMEM],
            [pltpu.VMEM((owned // 2, places), BF)],
            (10**9, 10**7),
            "cold_sum",
        )((rows_of * (owned // 2)).reshape(1), asked, grads)

    others = cold_sum(1 - core, incoming)
    hot_share = hot_share + swap(hot_share, "dp", 4)
    incoming = after(incoming, others, hot_share)
    mine = cold_sum(core, incoming)
    hot_share = paired(hot_share, swap(hot_share, "dp", 1), lax.axis_index("dp") % 2)
    mine = (mine + swap(others, "rep", 1)).astype(BF)
    mine = mine.astype(F32) + swap(mine, "rep", 2).astype(F32)
    hot_share = paired(hot_share, swap(hot_share, "rep", 2), lax.axis_index("rep") // 2)
    return tuple(paired(half, swap(half, "rep", 1), core) for half in (hot_share, mine))


def large_step(
    hot_ids, cold_rows, cold_owner, labels, hot_table, cold_table, cross_down, cross_up, cross_bias, out_weight
):
    rows = hot_ids.shape[0]
    n_data = lax.axis_size("dp")
    lookups = rows * NC
    capacity = 2 * ((lookups + n_data - 1) // n_data)
    owned = cold_table.shape[0]
    owner = cold_owner.reshape(lookups)
    local_row = cold_rows.reshape(lookups)
    onehot = (owner[:, None] == jnp.arange(n_data, dtype=jnp.int32)[None, :]).astype(jnp.int32)
    running = jnp.cumsum(onehot, axis=0)
    slot = jnp.sum(onehot * running, axis=1) - 1
    place = owner * capacity + slot
    requests = (
        jnp.full((n_data * capacity,), -1, jnp.int32)
        .at[place]
        .set(local_row)
        .reshape(n_data, capacity)
    )
    asked = lax.all_to_all(requests, "dp", split_axis=0, concat_axis=0, tiled=True)
    safe = jnp.maximum(asked, 0)
    found = jnp.take(cold_table, safe, axis=0).astype(jnp.bfloat16)
    found = jnp.where((asked >= 0)[:, :, None], found, jnp.zeros_like(found))
    returned = lax.all_to_all(found, "dp", split_axis=0, concat_axis=0, tiled=True)
    cold_emb = returned.reshape(n_data * capacity, E)[place].reshape(rows, NC, E)
    hot_emb = hot_table[hot_ids].astype(jnp.bfloat16)
    first = jnp.concatenate([hot_emb, cold_emb], axis=1).reshape(rows, F)
    down_full, up_full = (
        lax.all_gather(cross_down, ("dp", "rep"), axis=1, tiled=True),
        lax.all_gather(cross_up, ("dp", "rep"), axis=0, tiled=True),
    )
    hidden = jnp.dot(first, down_full, preferred_element_type=jnp.float32).astype(jnp.bfloat16)
    upper = jnp.dot(hidden, up_full, preferred_element_type=jnp.float32) + cross_bias[None, :]
    first_f = first.astype(jnp.float32)
    second = first_f * upper + first_f
    logit = jnp.sum(second * out_weight[None, :], axis=1)
    delta = jax.nn.sigmoid(logit) - labels.astype(jnp.float32)
    d_second = delta[:, None] * out_weight[None, :]
    d_upper = (d_second * first_f).astype(jnp.bfloat16)
    d_hidden = jnp.dot(d_upper, up_full.T, preferred_element_type=jnp.float32).astype(jnp.bfloat16)
    d_first = d_second * (upper + 1.0) + jnp.dot(
        d_hidden, down_full.T, preferred_element_type=jnp.float32
    )
    grads = d_first.reshape(rows, NH + NC, E)
    hot_partial = jax.ops.segment_sum(grads[:, :NH].reshape(rows * NH, E), hot_ids.reshape(-1), HOT)
    cold_low = grads[:, NH:].astype(jnp.bfloat16).reshape(lookups, E)
    outgoing = (
        jnp.zeros((n_data * capacity, E), jnp.bfloat16)
        .at[place]
        .set(cold_low)
        .reshape(n_data, capacity, E)
    )
    incoming = lax.all_to_all(outgoing, "dp", split_axis=0, concat_axis=0, tiled=True)
    flat_ids = asked.reshape(-1)
    segment = jnp.where(flat_ids >= 0, flat_ids, owned)
    cold_partial = jax.ops.segment_sum(
        incoming.reshape(n_data * capacity, E).astype(jnp.float32), segment, owned
    )
    return lax.psum(hot_partial, ("dp", "rep")), lax.psum(cold_partial, "rep")


def shards(
    hot_ids,
    cold_rows,
    cold_owner,
    labels,
    hot_table,
    hot_backup,
    cold_table,
    cold_backup,
    cross_down,
    cross_up,
    cross_bias,
    out_weight,
):
    rows = hot_ids.shape[0]
    owned = cold_table.shape[0]
    n_data = lax.axis_size("dp")
    n_reps = lax.axis_size("rep")
    step = small_step if is_small(n_data, n_reps) else large_step
    hot_grad, cold_grad = step(
        hot_ids,
        cold_rows,
        cold_owner,
        labels,
        hot_table,
        cold_table,
        cross_down,
        cross_up,
        cross_bias,
        out_weight,
    )
    batch_all = rows * n_data * n_reps
    rate_hot = 20.0 * math.sqrt(HOT / (batch_all * NH))
    rate_cold = 20.0 * math.sqrt(owned * n_data / (batch_all * NC))
    new_hot = compensate(hot_table, hot_backup, hot_grad, rate_hot)
    new_cold = compensate(cold_table, cold_backup, cold_grad, rate_cold)
    return (new_hot, new_cold)


def solution(mesh):
    placed = (
        P(("dp", "rep"), None),
        P(("dp", "rep"), None),
        P(("dp", "rep"), None),
        P(("dp", "rep")),
        P(),
        P(),
        P("dp", None),
        P("dp", None),
        P(None, ("dp", "rep")),
        P(("dp", "rep"), None),
        P(),
        P(),
    )
    return jax.shard_map(
        shards, mesh=mesh, in_specs=placed, out_specs=(P(), P("dp", None)), check_vma=False
    )
```
